32 devices in a mesh: sect: 4 (over y, core), dir: 8 (over z, x).
Axes of the slice: x: 2, y: 2, z: 4, core: 2. Of those that a mesh axis runs over, the one named last changes fastest.
Arguments:
- unknowns: bfloat16 [2, 8, 16, 128, 256], P(None, 'sect', 'dir'), may hold values from -6 to 6
- leaf_live: int32 [8, 16], P('sect', 'dir'), may hold values from 0 to 1, as said below
- near_blocks: bfloat16 [2, 8, 16, 9, 128, 128], P(None, 'sect', 'dir'), may hold values from -0.125 to 0.125
- aggregate: bfloat16 [2, 8, 16, 512, 128], P(None, 'sect', 'dir'), may hold values from -0.1875 to 0.1875
- disaggregate: bfloat16 [2, 8, 16, 128, 512], P(None, 'sect', 'dir'), may hold values from -0.1875 to 0.1875
- translate: float32 [16, 2, 512], P(None, None, 'dir'), may hold values from -1.2 to 1.2
Outputs:
- field: float32 [2, 8, 16, 128, 256], P(None, 'sect', 'dir')
The draws below stay inside these ranges and needn't reach their ends.
Inputs may be any that keep to these rules, and one draw needn't show every extreme that they name: `leaf_live`: every 2 x 2 block of leaves (one coarse box) has its first leaf live; in every draw some box has all four leaves live.
All inputs are finite; a program needn't handle non-finite values.
Results may differ from the reference program's by a relative error of at most 0.0036.
Values may be sent and summed in bfloat16 or wider, within the bound.
No kernel may reach another device: no remote copies, remote signals or barrier semaphores. Data moves between devices by JAX's collectives and lax.ppermute only.
A program may use at most 64 MiB of HBM per device.

```python
import jax
import jax.numpy as jnp
from jax import lax

LS = 128
Q = 512
R = 256
BROWS = 4
BCOLS = 8
LROWS = 8
LCOLS = 16


def draw_leaf_live(key, part):
    first_key, second_key, third_key = jax.random.split(jax.random.fold_in(key, 7), 3)
    random_live = jax.random.randint(first_key, (LROWS, LCOLS), 0, 2)
    row_index = jnp.arange(LROWS, dtype=jnp.int32)[:, None]
    col_index = jnp.arange(LCOLS, dtype=jnp.int32)[None, :]
    first_leaf = ((row_index % 2 == 0) & (col_index % 2 == 0)).astype(jnp.int32)
    full_row = jax.random.randint(second_key, (), 0, BROWS)
    full_col = jax.random.randint(third_key, (), 0, BCOLS)
    full_box = ((row_index // 2 == full_row) & (col_index // 2 == full_col)).astype(jnp.int32)
    return jnp.maximum(jnp.maximum(random_live, first_leaf), full_box).astype(jnp.int32)


def levels(stream_key, dims, shards, smallest, high):
    level, own = 1.0, jax.random.fold_in(stream_key, 6)
    for position, blocks in shards:
        steps = jnp.exp(jax.random.uniform(jax.random.fold_in(own, position), (blocks,), jnp.float32, smallest / len(shards), high / len(shards)))
        level = level * jnp.repeat(steps, dims[position] // blocks).reshape([-1 if axis == position else 1 for axis in range(len(dims))])
    return level


def gaussian(key, dims, width, bound, pieces=(), kind=jnp.bfloat16):
    array = jax.random.normal(key, dims, jnp.float32) * width
    if len(pieces) > 0:
        array = levels(key, dims, pieces, -0.22, 0.18) * array
    return jnp.clip(array, min=-bound, max=bound).astype(kind)


def setup_inputs(seed: int = 0) -> dict:
    keys = jax.random.split(jax.random.key(seed), 7)
    unknowns = gaussian(keys[0], (2, LROWS, LCOLS, LS, R), 1.0, 6.0, ((1, 4), (2, 8)))
    leaf_live = draw_leaf_live(jax.random.fold_in(keys[6], 71), 0)
    near_blocks = gaussian(keys[2], (2, LROWS, LCOLS, 9, LS, LS), (18 * LS) ** -0.5, 0.125, ((1, 4), (2, 8)))
    aggregate = gaussian(keys[3], (2, LROWS, LCOLS, Q, LS), (8 * LS) ** -0.5, 0.1875, ((1, 4), (2, 8)))
    disaggregate = gaussian(keys[4], (2, LROWS, LCOLS, LS, Q), (2 * Q) ** -0.5, 0.1875, ((1, 4), (2, 8)))
    translate = gaussian(keys[5], (16, 2, Q), 0.2, 1.2, ((2, 8),), jnp.float32)
    return dict(unknowns=unknowns, leaf_live=leaf_live, near_blocks=near_blocks, aggregate=aggregate, disaggregate=disaggregate, translate=translate)


far_offsets = [(row_step, col_step) for row_step in range(-2, 3) for col_step in range(-2, 3) if max(abs(row_step), abs(col_step)) == 2]


def complex_einsum(form, left, right):
    left = left.astype(jnp.float32)
    right = right.astype(jnp.float32)
    real = jnp.einsum(form, left[0], right[0]) - jnp.einsum(form, left[1], right[1])
    imag = jnp.einsum(form, left[0], right[1]) + jnp.einsum(form, left[1], right[0])
    return jnp.stack([real, imag])


def reference(unknowns, leaf_live, near_blocks, aggregate, disaggregate, translate):
    live = leaf_live.astype(jnp.float32)[None, :, :, None, None]
    masked = (unknowns.astype(jnp.float32) * live).astype(jnp.bfloat16)
    padded = jnp.pad(masked, ((0, 0), (1, 1), (1, 1), (0, 0), (0, 0)))
    near = jnp.zeros(unknowns.shape, jnp.float32)
    for row_step in range(-1, 2):
        for col_step in range(-1, 2):
            which = (row_step + 1) * 3 + col_step + 1
            beside = padded[:, 1 + row_step:1 + row_step + LROWS, 1 + col_step:1 + col_step + LCOLS]
            near = near + complex_einsum("ijmn,ijnr->ijmr", near_blocks[:, :, :, which], beside)
    agg_view = aggregate.reshape(2, BROWS, 2, BCOLS, 2, Q, LS)
    leaf_view = masked.reshape(2, BROWS, 2, BCOLS, 2, LS, R)
    patterns = complex_einsum("aubvqn,aubvnr->abqr", agg_view, leaf_view).astype(jnp.bfloat16)
    source = jnp.pad(patterns.astype(jnp.float32), ((0, 0), (0, 0), (2, 2), (0, 0), (0, 0)))
    rows_in = []
    for target in range(BROWS):
        total = jnp.zeros((2, BCOLS, Q, R), jnp.float32)
        for row_step in range(-2, 3):
            anchor = target + row_step
            if 0 <= anchor < BROWS:
                term = jnp.zeros((2, BCOLS, Q, R), jnp.float32)
                for index, (step_row, step_col) in enumerate(far_offsets):
                    if step_row == row_step:
                        shifted = source[:, anchor, 2 + step_col:2 + step_col + BCOLS]
                        coef_real = translate[index, 0][None, :, None]
                        coef_imag = translate[index, 1][None, :, None]
                        real = coef_real * shifted[0] - coef_imag * shifted[1]
                        imag = coef_real * shifted[1] + coef_imag * shifted[0]
                        term = term + jnp.stack([real, imag])
                rounded = lax.optimization_barrier(term.astype(jnp.bfloat16))
                total = total + rounded.astype(jnp.float32)
        rows_in.append(total.astype(jnp.bfloat16))
    incoming = jnp.stack(rows_in, axis=1)
    dis_view = disaggregate.reshape(2, BROWS, 2, BCOLS, 2, LS, Q)
    far = complex_einsum("aubvmq,abqr->aubvmr", dis_view, incoming).reshape(2, LROWS, LCOLS, LS, R)
    return (near + far) * live
```

```python
import functools

import jax
import jax.numpy as jnp
from jax import lax
from jax.experimental import pallas as pl
from jax.experimental.pallas import tpu as pltpu
from jax.sharding import PartitionSpec as P

REACH = 2
PAIR = 2
MIB = 1 << 20
far_offsets = [
    (row_step, col_step)
    for row_step in range(-REACH, REACH + 1)
    for col_step in range(-REACH, REACH + 1)
    if max(abs(row_step), abs(col_step)) == REACH
]
VMEM = pl.BlockSpec(memory_space=pltpu.VMEM)
SMEM = pl.BlockSpec(memory_space=pltpu.SMEM)


def params(mib):
    return pltpu.CompilerParams(vmem_limit_bytes=mib * MIB)


def swap_pairs(count, first):
    pairs = []
    for i in range(count):
        partner = i + 1 if (i - first) % 2 == 0 else i - 1
        pairs.append((i, partner if 0 <= partner < count else i))
    return pairs


def column_kernel(live_ref, unknowns_ref, near_ref, cross_ref):
    odd = lax.rem(lax.axis_index("dir"), 2)
    for u in range(unknowns_ref.shape[1]):
        for out_ref, v in ((near_ref, 1 - odd), (cross_ref, odd)):
            keep = live_ref[u, v].astype(jnp.float32).astype(jnp.bfloat16)
            out_ref[:, u] = unknowns_ref[:, u, v] * keep


def complex_dot(left_real, left_imag, right):
    rows = left_real.shape[0]
    cols = right.shape[1] // 2
    both = jnp.dot(
        jnp.concatenate([left_real, left_imag], axis=0), right, preferred_element_type=jnp.float32
    )
    real = both[:rows, :cols] - both[rows:, cols:]
    imag = both[:rows, cols:] + both[rows:, :cols]
    return real, imag


def pattern_kernel(live_ref, unknowns_ref, aggregate_ref, out_ref, leaves_ref):
    parts, _, narrow, sides = out_ref.shape
    size = unknowns_ref.shape[3]
    width = unknowns_ref.shape[2]

    @pl.when(pl.program_id(0) == 0)
    def _():
        for u in range(unknowns_ref.shape[1]):
            for v in range(width):
                keep = live_ref[u, v].astype(jnp.float32).astype(jnp.bfloat16)
                at = (u * width + v) * size
                for c in range(2):
                    leaves_ref[at : at + size, c * sides : (c + 1) * sides] = (
                        unknowns_ref[c, u, v] * keep
                    )

    left = [
        jnp.concatenate(
            [
                aggregate_ref[c, u, v]
                for u in range(unknowns_ref.shape[1])
                for v in range(width)
            ],
            axis=1,
        )
        for c in range(2)
    ]
    real, imag = complex_dot(left[0], left[1], leaves_ref[...])
    for part in range(parts):
        out_ref[part, 0] = real[part * narrow : (part + 1) * narrow].astype(jnp.bfloat16)
        out_ref[part, 1] = imag[part * narrow : (part + 1) * narrow].astype(jnp.bfloat16)


def translate_kernel(groups, own_ref, even_ref, odd_ref, coef_ref, out_ref, beside_ref, wide_ref):
    box_rows = own_ref.shape[0] // PAIR
    depth, sides = own_ref.shape[2], own_ref.shape[3]
    lanes = min(128, sides)
    group = lax.axis_index("dir") // PAIR
    parity = lax.rem(group, 2)
    for ref, slot, missing in (
        (even_ref, 1 - parity, (parity == 0) & (group == groups - 1)),
        (odd_ref, parity, (group == 0) | ((parity == 1) & (group == groups - 1))),
    ):

        @pl.when(missing)
        def _():
            beside_ref[slot] = jnp.zeros_like(ref)

        @pl.when(jnp.logical_not(missing))
        def _():
            beside_ref[slot] = ref[...]

    coefs = coef_ref[...]
    for index in range(coefs.shape[1]):
        wide_ref[index] = jnp.broadcast_to(coefs[:, index : index + 1], (depth, lanes))

    for lane in range(0, sides, lanes):
        span = slice(lane, lane + lanes)
        totals = {}
        for source in range(box_rows):
            held = []
            for col in range(-REACH, PAIR + REACH):
                at = source * PAIR + col % PAIR
                if col < 0:
                    held.append([beside_ref[0, at, c, :, span].astype(jnp.float32) for c in range(2)])
                elif col >= PAIR:
                    held.append([beside_ref[1, at, c, :, span].astype(jnp.float32) for c in range(2)])
                else:
                    held.append([own_ref[at, c, :, span].astype(jnp.float32) for c in range(2)])
            for target in range(max(0, source - REACH), min(box_rows, source + REACH + 1)):
                for col in range(PAIR):
                    real = imag = None
                    for index, (row_step, col_step) in enumerate(far_offsets):
                        if row_step != source - target:
                            continue
                        coef_real, coef_imag = wide_ref[2 * index], wide_ref[2 * index + 1]
                        from_real, from_imag = held[col + col_step + REACH]
                        term_real = coef_real * from_real - coef_imag * from_imag
                        term_imag = coef_real * from_imag + coef_imag * from_real
                        real = term_real if real is None else real + term_real
                        imag = term_imag if imag is None else imag + term_imag
                    real = real.astype(jnp.bfloat16).astype(jnp.float32)
                    imag = imag.astype(jnp.bfloat16).astype(jnp.float32)
                    if (target, col) in totals:
                        old = totals[target, col]
                        totals[target, col] = (old[0] + real, old[1] + imag)
                    else:
                        totals[target, col] = (real, imag)
        for (target, col), (real, imag) in totals.items():
            out_ref[target * PAIR + col, 0, :, span] = real.astype(jnp.bfloat16)
            out_ref[target * PAIR + col, 1, :, span] = imag.astype(jnp.bfloat16)


def row_kernel(near_ref, cross_ref, from_near_ref, from_cross_ref, out_near_ref, out_cross_ref):
    odd = lax.rem(lax.axis_index("sect"), 2)
    for slot, ref in enumerate((near_ref, cross_ref, from_near_ref, from_cross_ref)):
        out_near_ref[:, slot] = ref[:, 1 - odd]
        out_cross_ref[:, slot] = ref[:, odd]


def near_kernel(
    near_ref, cross_ref, from_near_ref, from_cross_ref, row_near_ref, row_cross_ref, blocks_ref,
    out_ref, grid_ref,
):
    size, sides = near_ref.shape[2], near_ref.shape[3]
    deep = near_ref.shape[1]
    wide = 2
    leaf = pl.program_id(0)

    @pl.when(leaf == 0)
    def _():
        col_at, col_count = lax.axis_index("dir"), lax.axis_size("dir")
        row_at, row_count = lax.axis_index("sect"), lax.axis_size("sect")
        col_odd, row_odd = lax.rem(col_at, 2), lax.rem(row_at, 2)
        columns = (2 - col_odd, 1 + col_odd, 3 - 3 * col_odd, 3 * col_odd)
        no_col = ((col_odd == 0) & (col_at == 0)) | ((col_odd == 1) & (col_at == col_count - 1))
        no_row = ((row_odd == 0) & (row_at == 0)) | ((row_odd == 1) & (row_at == row_count - 1))
        for slot, ref in enumerate((near_ref, cross_ref, from_near_ref, from_cross_ref)):
            for u in range(deep):
                for c in range(2):
                    grid_ref[1 + u, columns[slot], :, c * sides : (c + 1) * sides] = ref[c, u]
            for c in range(2):
                half = slice(c * sides, (c + 1) * sides)
                grid_ref[3 - 3 * row_odd, columns[slot], :, half] = row_near_ref[c, slot]
                grid_ref[3 * row_odd, columns[slot], :, half] = row_cross_ref[c, slot]

        @pl.when(no_col)
        def _():
            for i in range(deep + 2):
                grid_ref[i, columns[3]] = jnp.zeros(grid_ref.shape[2:], grid_ref.dtype)

        @pl.when(no_row)
        def _():
            for j in range(wide + 2):
                grid_ref[3 * row_odd, j] = jnp.zeros(grid_ref.shape[2:], grid_ref.dtype)

    u, v = leaf // wide, lax.rem(leaf, wide)
    right = jnp.concatenate(
        [grid_ref[u + a, v + b] for a in range(3) for b in range(3)], axis=0
    )
    left = [jnp.concatenate([blocks_ref[c, 0, 0, k] for k in range(9)], axis=1) for c in range(2)]
    real, imag = complex_dot(left[0], left[1], right)
    out_ref[0, 0, 0] = real
    out_ref[1, 0, 0] = imag


def far_kernel(live_ref, incoming_ref, disaggregate_ref, near_ref, out_ref, right_ref):
    parts, _, narrow, sides = incoming_ref.shape
    leaf = pl.program_id(0)
    wide = live_ref.shape[1]

    @pl.when(leaf == 0)
    def _():
        for part in range(parts):
            for c in range(2):
                right_ref[part * narrow : (part + 1) * narrow, c * sides : (c + 1) * sides] = (
                    incoming_ref[part, c]
                )

    live = live_ref[leaf // wide, lax.rem(leaf, wide)].astype(jnp.float32)
    real, imag = complex_dot(
        disaggregate_ref[0, 0, 0], disaggregate_ref[1, 0, 0], right_ref[...]
    )
    out_ref[0, 0, 0] = (near_ref[0, 0, 0] + real) * live
    out_ref[1, 0, 0] = (near_ref[1, 0, 0] + imag) * live


def direction_coefs(translate, narrow):
    sect_count, dir_count = lax.axis_size("sect"), lax.axis_size("dir")
    groups = dir_count // PAIR
    held = translate.shape[2]
    pieces = narrow // held
    got = []
    for turn in range(pieces):
        sends = []
        for sect in range(sect_count):
            for col in range(dir_count):
                group, block = col // PAIR, sect * PAIR + col % PAIR
                shard = block * pieces + (turn + group // sect_count) % pieces
                sends.append(((group % sect_count) * dir_count + shard, sect * dir_count + col))
        got.append(lax.ppermute(translate, ("sect", "dir"), sends))
    if pieces == 1:
        return got[0]
    first = lax.axis_index("dir") // PAIR // sect_count
    return jnp.concatenate(
        [
            lax.dynamic_index_in_dim(
                jnp.stack(got), lax.rem(piece - first + pieces, pieces), 0, keepdims=False
            )
            for piece in range(pieces)
        ],
        axis=2,
    )


def shards(unknowns, leaf_live, near_blocks, aggregate, disaggregate, translate):
    sect_count, dir_count = lax.axis_size("sect"), lax.axis_size("dir")
    _, deep, wide, size, sides = unknowns.shape
    total_dirs = aggregate.shape[3]
    groups = dir_count // PAIR
    parts = sect_count * PAIR
    narrow = total_dirs // parts
    bf16, f32 = jnp.bfloat16, jnp.float32
    members = [
        [sect * dir_count + group * PAIR + col for sect in range(sect_count) for col in range(PAIR)]
        for group in range(groups)
    ]

    def spread(array):
        return lax.all_to_all(
            array, ("sect", "dir"), split_axis=0, concat_axis=0, tiled=True, axis_index_groups=members
        )

    def swap(array, axis, first, width=1):
        count = lax.axis_size(axis) // width
        return lax.ppermute(
            array,
            axis,
            [(i * width + j, k * width + j) for i, k in swap_pairs(count, first) for j in range(width)],
        )

    column = jax.ShapeDtypeStruct((2, deep, size, sides), bf16)
    col_near, col_cross = pl.pallas_call(
        column_kernel,
        in_specs=[SMEM, VMEM],
        out_specs=[VMEM, VMEM],
        out_shape=[column, column],
        compiler_params=params(8),
        name="columns",
    )(leaf_live, unknowns)
    from_cross = swap(col_cross, "dir", 1)

    steps = 2
    patterns = pl.pallas_call(
        pattern_kernel,
        grid=(steps,),
        in_specs=[
            SMEM,
            pl.BlockSpec(unknowns.shape, lambda i: (0, 0, 0, 0, 0)),
            pl.BlockSpec((2, deep, wide, total_dirs // steps, size), lambda i: (0, 0, 0, i, 0)),
        ],
        out_specs=pl.BlockSpec((parts // steps, 2, narrow, sides), lambda i: (i, 0, 0, 0)),
        out_shape=jax.ShapeDtypeStruct((parts, 2, narrow, sides), bf16),
        scratch_shapes=[pltpu.VMEM((deep * wide * size, 2 * sides), bf16)],
        compiler_params=params(16),
        name="patterns",
    )(leaf_live, unknowns, aggregate)
    own = spread(patterns)
    coefs = direction_coefs(translate, narrow).reshape(2 * len(far_offsets), narrow).T
    from_near = swap(col_near, "dir", 0)
    even = swap(own, "dir", 0, PAIR)
    odd = swap(own, "dir", 1, PAIR)

    row = jax.ShapeDtypeStruct((2, 4, size, sides), bf16)
    row_near, row_cross = pl.pallas_call(
        row_kernel,
        in_specs=[VMEM] * 4,
        out_specs=[VMEM] * 2,
        out_shape=[row, row],
        compiler_params=params(8),
        name="rows",
    )(col_near, col_cross, from_near, from_cross)
    row_near = swap(row_near, "sect", 0)
    row_cross = swap(row_cross, "sect", 1)

    depth = 16
    block = pl.BlockSpec((parts, 2, depth, sides), lambda i: (0, 0, i, 0))
    incoming = pl.pallas_call(
        functools.partial(translate_kernel, groups),
        grid=(narrow // depth,),
        in_specs=[block, block, block, pl.BlockSpec((depth, coefs.shape[1]), lambda i: (i, 0))],
        out_specs=block,
        out_shape=jax.ShapeDtypeStruct(own.shape, bf16),
        scratch_shapes=[
            pltpu.VMEM((2, parts, 2, depth, sides), bf16),
            pltpu.VMEM((coefs.shape[1], depth, min(128, sides)), f32),
        ],
        compiler_params=params(16),
        name="translations",
    )(own, even, odd, coefs)
    returned = spread(incoming)

    leaf_out = pl.BlockSpec((2, 1, 1, size, sides), lambda i: (0, i // wide, i % wide, 0, 0))
    field = jax.ShapeDtypeStruct(unknowns.shape, f32)
    near = pl.pallas_call(
        near_kernel,
        grid=(deep * wide,),
        in_specs=[VMEM] * 6
        + [pl.BlockSpec((2, 1, 1, 9, size, size), lambda i: (0, i // wide, i % wide, 0, 0, 0))],
        out_specs=leaf_out,
        out_shape=field,
        scratch_shapes=[pltpu.VMEM((deep + 2, wide + 2, size, 2 * sides), bf16)],
        compiler_params=params(24),
        name="near",
    )(col_near, col_cross, from_near, from_cross, row_near, row_cross, near_blocks)
    return pl.pallas_call(
        far_kernel,
        grid=(deep * wide,),
        in_specs=[
            SMEM,
            VMEM,
            pl.BlockSpec((2, 1, 1, size, total_dirs), lambda i: (0, i // wide, i % wide, 0, 0)),
            leaf_out,
        ],
        out_specs=leaf_out,
        out_shape=field,
        scratch_shapes=[pltpu.VMEM((total_dirs, 2 * sides), bf16)],
        compiler_params=params(16),
        name="far",
    )(leaf_live, returned, disaggregate, near)


def solution(mesh):
    in_specs = (
        P(None, "sect", "dir", None, None),
        P("sect", "dir"),
        P(None, "sect", "dir", None, None, None),
        P(None, "sect", "dir", None, None),
        P(None, "sect", "dir", None, None),
        P(None, None, "dir"),
    )
    out_specs = P(None, "sect", "dir", None, None)
    return jax.shard_map(shards, mesh=mesh, in_specs=in_specs, out_specs=out_specs, check_vma=False)
```

```python
import functools

import jax
import jax.numpy as jnp
from jax import lax
from jax.experimental import pallas as pl
from jax.experimental.pallas import tpu as pltpu
from jax.sharding import PartitionSpec as P

REACH = 2
PAIR = 2
MIB = 1 << 20
far_offsets = [
    (row_step, col_step)
    for row_step in range(-REACH, REACH + 1)
    for col_step in range(-REACH, REACH + 1)
    if max(abs(row_step), abs(col_step)) == REACH
]
VMEM = pl.BlockSpec(memory_space=pltpu.VMEM)
SMEM = pl.BlockSpec(memory_space=pltpu.SMEM)
ANY = pl.BlockSpec(memory_space=pl.ANY)


def params(mib=56):
    return pltpu.CompilerParams(vmem_limit_bytes=mib * MIB)


def cost(micros):
    return pl.CostEstimate(flops=int(micros * 1.15e9), bytes_accessed=int(micros * 3.69e6), transcendentals=0)


def swap_pairs(count, first):
    pairs = []
    for i in range(count):
        partner = i + 1 if (i - first) % 2 == 0 else i - 1
        pairs.append((i, partner if 0 <= partner < count else None))
    return pairs


def swap_cols(array, first, width=1):
    rows, cols = lax.axis_size("sect"), lax.axis_size("dir")
    sends = []
    for row in range(rows):
        for group, partner in swap_pairs(cols // width, first):
            for col in range(width):
                to = (
                    (row ^ 1) * cols + group * width + col
                    if partner is None
                    else row * cols + partner * width + col
                )
                sends.append((row * cols + group * width + col, to))
    return lax.ppermute(array, ("sect", "dir"), sends)


def swap_rows(array, first):
    rows = lax.axis_size("sect")
    return lax.ppermute(
        array,
        "sect",
        [(row, rows - 1 - row if partner is None else partner) for row, partner in swap_pairs(rows, first)],
    )


def complex_dot(left_real, left_imag, right):
    rows = left_real.shape[0]
    cols = right.shape[1] // 2
    both = jnp.dot(
        jnp.concatenate([left_real, left_imag], axis=0), right, preferred_element_type=jnp.float32
    )
    real = both[:rows, :cols] - both[rows:, cols:]
    imag = both[:rows, cols:] + both[rows:, :cols]
    return real, imag


def pattern_kernel(
    live_ref, unknowns_ref, aggregate_ref, out_ref, near_ref, cross_ref, leaves_ref,
):
    parts, _, narrow, sides = out_ref.shape
    deep, wide, size = unknowns_ref.shape[1:4]

    @pl.when(pl.program_id(0) == 0)
    def _():
        for u in range(deep):
            for v in range(wide):
                keep = live_ref[u, v].astype(jnp.float32).astype(jnp.bfloat16)
                at = (u * wide + v) * size
                for c in range(2):
                    leaves_ref[at : at + size, c * sides : (c + 1) * sides] = (
                        unknowns_ref[c, u, v] * keep
                    )

    left = [
        jnp.concatenate([aggregate_ref[c, u, v] for u in range(deep) for v in range(wide)], axis=1)
        for c in range(2)
    ]
    real, imag = complex_dot(left[0], left[1], leaves_ref[...])
    for part in range(parts):
        out_ref[part, 0] = real[part * narrow : (part + 1) * narrow].astype(jnp.bfloat16)
        out_ref[part, 1] = imag[part * narrow : (part + 1) * narrow].astype(jnp.bfloat16)

    @pl.when(pl.program_id(0) == 0)
    def _():
        odd = lax.rem(lax.axis_index("dir"), 2)

        def leaf(u, v, c):
            at = pl.multiple_of((u * wide + v) * size, size)
            return leaves_ref[pl.ds(at, size), c * sides : (c + 1) * sides]

        for c in range(2):
            for u in range(deep):
                near_ref[c, u] = leaf(u, 1 - odd, c)
                cross_ref[c, u] = leaf(u, odd, c)


def translate_kernel(
    groups, own_ref, even_ref, odd_ref, coef_ref, out_ref, held_ref, made_ref, coefs_ref, wide_ref,
    coef_sem, in_sem, out_sem,
):
    parts, _, narrow, sides = own_ref.shape
    box_rows = parts // PAIR
    depth, lanes = min(16, narrow), min(128, sides)
    group = lax.axis_index("dir") // PAIR
    parity = lax.rem(group, 2)
    no_even = (parity == 0) & (group == groups - 1)
    no_odd = (group == 0) | ((parity == 1) & (group == groups - 1))
    sources = ((own_ref, 2, None), (even_ref, 1 - parity, no_even), (odd_ref, parity, no_odd))

    def span(at):
        return pl.ds(pl.multiple_of(at * depth, depth), depth)

    def arrival(which, at):
        ref, slot, _ = sources[which]
        return pltpu.make_async_copy(
            ref.at[:, :, span(at)], held_ref.at[slot, :, :, span(at)], in_sem.at[which, at]
        )

    def departure(at):
        return pltpu.make_async_copy(
            made_ref.at[:, :, span(at)], out_ref.at[:, :, span(at)], out_sem.at[at]
        )

    coefs_here = pltpu.make_async_copy(coef_ref, coefs_ref, coef_sem)
    coefs_here.start()
    for at in range(narrow // depth):
        for which in range(3):
            arrival(which, at).start()

    coefs_here.wait()
    coefs = coefs_ref[...].T
    for index in range(coefs.shape[1]):
        wide_ref[index] = jnp.broadcast_to(coefs[:, index : index + 1], (narrow, lanes))

    def chunk(at, carry):
        for which in range(3):
            arrival(which, at).wait()
        for _, slot, missing in sources[1:]:

            @pl.when(missing)
            def _():
                held_ref[slot, :, :, span(at)] = jnp.zeros((parts, 2, depth, sides), held_ref.dtype)

        def tile(place, carry):
            across = pl.ds(pl.multiple_of(place * lanes, lanes), lanes)
            for col in range(PAIR):
                totals = {}
                for source in range(box_rows):
                    held = {}
                    for step in range(-REACH, REACH + 1):
                        slot = 0 if col + step < 0 else 1 if col + step >= PAIR else 2
                        box = source * PAIR + (col + step) % PAIR
                        held[step] = [
                            held_ref[slot, box, c, span(at), across].astype(jnp.float32)
                            for c in range(2)
                        ]
                    for target in range(max(0, source - REACH), min(box_rows, source + REACH + 1)):
                        real = imag = None
                        for index, (row_step, step) in enumerate(far_offsets):
                            if row_step != source - target:
                                continue
                            coef_real = wide_ref[2 * index, span(at)]
                            coef_imag = wide_ref[2 * index + 1, span(at)]
                            from_real, from_imag = held[step]
                            term_real = coef_real * from_real - coef_imag * from_imag
                            term_imag = coef_real * from_imag + coef_imag * from_real
                            real = term_real if real is None else real + term_real
                            imag = term_imag if imag is None else imag + term_imag
                        real = real.astype(jnp.bfloat16).astype(jnp.float32)
                        imag = imag.astype(jnp.bfloat16).astype(jnp.float32)
                        if target in totals:
                            old = totals[target]
                            totals[target] = (old[0] + real, old[1] + imag)
                        else:
                            totals[target] = (real, imag)
                for target, total in totals.items():
                    for c in range(2):
                        made_ref[target * PAIR + col, c, span(at), across] = total[c].astype(jnp.bfloat16)
            return carry

        lax.fori_loop(0, sides // lanes, tile, 0, unroll=True)
        departure(at).start()
        return carry

    lax.fori_loop(0, narrow // depth, chunk, 0)
    for at in range(narrow // depth):
        departure(at).wait()


def row_kernel(near_ref, cross_ref, from_cross_ref, out_near_ref, out_cross_ref):
    odd = lax.rem(lax.axis_index("sect"), 2)
    for slot, ref in enumerate((near_ref, cross_ref, from_cross_ref)):
        out_near_ref[:, slot] = ref[:, 1 - odd]
        out_cross_ref[:, slot] = ref[:, odd]


def column_kernel(near_ref, row_near_ref, row_cross_ref, out_ref):
    deep = near_ref.shape[1]
    out_ref[:, :deep] = near_ref[...]
    out_ref[:, deep] = row_near_ref[:, 0]
    out_ref[:, deep + 1] = row_cross_ref[:, 0]


def near_kernel(
    near_ref, cross_ref, from_cross_ref, from_near_ref, row_near_ref, row_cross_ref, blocks_ref,
    out_ref, grid_ref,
):
    sides = near_ref.shape[3]
    deep = near_ref.shape[1]
    wide = 2
    leaf = pl.program_id(0)

    @pl.when(leaf == 0)
    def _():
        col_at, col_count = lax.axis_index("dir"), lax.axis_size("dir")
        row_at, row_count = lax.axis_index("sect"), lax.axis_size("sect")
        col_odd, row_odd = lax.rem(col_at, 2), lax.rem(row_at, 2)
        columns = (2 - col_odd, 1 + col_odd, 3 * col_odd, 3 - 3 * col_odd)
        row_next, row_last = 3 - 3 * row_odd, 3 * row_odd
        no_col = ((col_odd == 0) & (col_at == 0)) | ((col_odd == 1) & (col_at == col_count - 1))
        no_row = ((row_odd == 0) & (row_at == 0)) | ((row_odd == 1) & (row_at == row_count - 1))
        for slot, ref in enumerate((near_ref, cross_ref, from_cross_ref, from_near_ref)):
            for c in range(2):
                half = slice(c * sides, (c + 1) * sides)
                for u in range(deep):
                    grid_ref[1 + u, columns[slot], :, half] = ref[c, u]
                if slot < 3:
                    grid_ref[row_next, columns[slot], :, half] = row_near_ref[c, slot]
                    grid_ref[row_last, columns[slot], :, half] = row_cross_ref[c, slot]
                else:
                    grid_ref[row_next, columns[slot], :, half] = ref[c, deep]
                    grid_ref[row_last, columns[slot], :, half] = ref[c, deep + 1]

        @pl.when(no_col)
        def _():
            for i in range(deep + 2):
                grid_ref[i, columns[2]] = jnp.zeros(grid_ref.shape[2:], grid_ref.dtype)

        @pl.when(no_row)
        def _():
            for j in range(wide + 2):
                grid_ref[row_last, j] = jnp.zeros(grid_ref.shape[2:], grid_ref.dtype)

    u, v = leaf // wide, lax.rem(leaf, wide)
    right = jnp.concatenate(
        [grid_ref[u + a, v + b] for a in range(3) for b in range(3)], axis=0
    )
    left = [jnp.concatenate([blocks_ref[c, 0, 0, k] for k in range(9)], axis=1) for c in range(2)]
    real, imag = complex_dot(left[0], left[1], right)
    out_ref[0, 0, 0] = real
    out_ref[1, 0, 0] = imag


def far_kernel(
    live_ref, incoming_ref, disaggregate_ref, near_ref, out_ref, right_ref, made_ref, in_sem, out_sem
):
    parts, _, narrow, sides = incoming_ref.shape
    deep, wide = live_ref.shape

    def arrival(part, c):
        return pltpu.make_async_copy(
            incoming_ref.at[part, c],
            right_ref.at[part * narrow : (part + 1) * narrow, c * sides : (c + 1) * sides],
            in_sem.at[part, c],
        )

    def departure(u, v):
        return pltpu.make_async_copy(
            made_ref.at[:, u, v], out_ref.at[:, u, v], out_sem.at[u, v]
        )

    for part in range(parts):
        for c in range(2):
            arrival(part, c).start()
    for part in range(parts):
        for c in range(2):
            arrival(part, c).wait()
    for u in range(deep):
        for v in range(wide):
            live = live_ref[u, v].astype(jnp.float32)
            real, imag = complex_dot(
                disaggregate_ref[0, u, v], disaggregate_ref[1, u, v], right_ref[...]
            )
            made_ref[0, u, v] = (near_ref[0, u, v] + real) * live
            made_ref[1, u, v] = (near_ref[1, u, v] + imag) * live
            departure(u, v).start()
    for u in range(deep):
        for v in range(wide):
            departure(u, v).wait()


def direction_coefs(translate, narrow):
    sect_count, dir_count = lax.axis_size("sect"), lax.axis_size("dir")
    groups = dir_count // PAIR
    held = translate.shape[2]
    pieces = narrow // held
    got = []
    for turn in range(pieces):
        sends = []
        for sect in range(sect_count):
            for col in range(dir_count):
                group, block = col // PAIR, sect * PAIR + col % PAIR
                shard = block * pieces + (turn + group // sect_count) % pieces
                sends.append(((group % sect_count) * dir_count + shard, sect * dir_count + col))
        got.append(lax.ppermute(translate, ("sect", "dir"), sends))
    if pieces == 1:
        return got[0]
    first = lax.axis_index("dir") // PAIR // sect_count
    return jnp.concatenate(
        [
            lax.dynamic_index_in_dim(
                jnp.stack(got), lax.rem(piece - first + pieces, pieces), 0, keepdims=False
            )
            for piece in range(pieces)
        ],
        axis=2,
    )


def shards(unknowns, leaf_live, near_blocks, aggregate, disaggregate, translate):
    sect_count, dir_count = lax.axis_size("sect"), lax.axis_size("dir")
    _, deep, wide, size, sides = unknowns.shape
    total_dirs = aggregate.shape[3]
    groups = dir_count // PAIR
    parts = sect_count * PAIR
    narrow = total_dirs // parts
    bf16, f32 = jnp.bfloat16, jnp.float32
    members = [
        [sect * dir_count + group * PAIR + col for sect in range(sect_count) for col in range(PAIR)]
        for group in range(groups)
    ]

    def spread(array):
        return lax.all_to_all(
            array, ("sect", "dir"), split_axis=0, concat_axis=0, tiled=True, axis_index_groups=members
        )

    column = jax.ShapeDtypeStruct((2, deep, size, sides), bf16)
    steps = 2
    whole = [pl.BlockSpec(a.shape, lambda i, n=len(a.shape): (0,) * n) for a in (unknowns, column)]
    patterns, col_near, col_cross = pl.pallas_call(
        pattern_kernel,
        grid=(steps,),
        in_specs=[
            SMEM,
            whole[0],
            pl.BlockSpec((2, deep, wide, total_dirs // steps, size), lambda i: (0, 0, 0, i, 0)),
        ],
        out_specs=[
            pl.BlockSpec((parts // steps, 2, narrow, sides), lambda i: (i, 0, 0, 0)),
            whole[1],
            whole[1],
        ],
        out_shape=[jax.ShapeDtypeStruct((parts, 2, narrow, sides), bf16), column, column],
        scratch_shapes=[pltpu.VMEM((deep * wide * size, 2 * sides), bf16)],
        compiler_params=params(),
        name="patterns",
    )(leaf_live, unknowns, aggregate)
    from_cross = swap_cols(col_cross, 1)
    row = jax.ShapeDtypeStruct((2, 3, size, sides), bf16)
    row_near, row_cross = pl.pallas_call(
        row_kernel,
        in_specs=[VMEM] * 3,
        out_specs=[VMEM] * 2,
        out_shape=[row, row],
        compiler_params=params(16),
        cost_estimate=cost(4000),
        name="rows",
    )(col_near, col_cross, from_cross)
    translate, _ = lax.optimization_barrier((translate, row_cross))
    coefs = direction_coefs(translate, narrow)
    own = spread(patterns)
    own, _, _ = lax.optimization_barrier((own, row_near, row_cross))
    row_near = swap_rows(row_near, 0)
    row_cross = swap_rows(row_cross, 1)
    even = swap_cols(own, 0, PAIR)
    odd = swap_cols(own, 1, PAIR)
    tall = pl.pallas_call(
        column_kernel,
        in_specs=[VMEM] * 3,
        out_specs=VMEM,
        out_shape=jax.ShapeDtypeStruct((2, deep + 2, size, sides), bf16),
        compiler_params=params(16),
        cost_estimate=cost(4000),
        name="columns",
    )(col_near, row_near, row_cross)
    from_near = swap_cols(tall, 0)
    even, odd, coefs, _ = lax.optimization_barrier((even, odd, coefs, tall))
    coefs = coefs.reshape(2 * len(far_offsets), narrow)

    chunks = narrow // min(16, narrow)
    incoming = pl.pallas_call(
        functools.partial(translate_kernel, groups),
        in_specs=[ANY] * 4,
        out_specs=ANY,
        out_shape=jax.ShapeDtypeStruct(own.shape, bf16),
        scratch_shapes=[
            pltpu.VMEM((3, *own.shape), bf16),
            pltpu.VMEM(own.shape, bf16),
            pltpu.VMEM(coefs.shape, f32),
            pltpu.VMEM((2 * len(far_offsets), narrow, min(128, sides)), f32),
            pltpu.SemaphoreType.DMA,
            pltpu.SemaphoreType.DMA((3, chunks)),
            pltpu.SemaphoreType.DMA((chunks,)),
        ],
        compiler_params=params(16),
        cost_estimate=cost(4000),
        name="translations",
    )(own, even, odd, coefs)
    returned = spread(incoming)

    leaf_out = pl.BlockSpec((2, 1, 1, size, sides), lambda i: (0, i // wide, i % wide, 0, 0))
    field = jax.ShapeDtypeStruct(unknowns.shape, f32)
    near = pl.pallas_call(
        near_kernel,
        grid=(deep * wide,),
        in_specs=[VMEM] * 6
        + [pl.BlockSpec((2, 1, 1, 9, size, size), lambda i: (0, i // wide, i % wide, 0, 0, 0))],
        out_specs=leaf_out,
        out_shape=field,
        scratch_shapes=[pltpu.VMEM((deep + 2, wide + 2, size, 2 * sides), bf16)],
        compiler_params=params(16),
        cost_estimate=cost(4000),
        name="near",
    )(
        col_near, col_cross, from_cross, from_near, row_near, row_cross, near_blocks,
    )
    return pl.pallas_call(
        far_kernel,
        in_specs=[SMEM, ANY, VMEM, VMEM],
        out_specs=ANY,
        out_shape=field,
        scratch_shapes=[
            pltpu.VMEM((total_dirs, 2 * sides), bf16),
            pltpu.VMEM(unknowns.shape, f32),
            pltpu.SemaphoreType.DMA((parts, 2)),
            pltpu.SemaphoreType.DMA((deep, wide)),
        ],
        compiler_params=params(16),
        name="far",
    )(leaf_live, returned, disaggregate, near)


def solution(mesh):
    in_specs = (
        P(None, "sect", "dir", None, None),
        P("sect", "dir"),
        P(None, "sect", "dir", None, None, None),
        P(None, "sect", "dir", None, None),
        P(None, "sect", "dir", None, None),
        P(None, None, "dir"),
    )
    out_specs = P(None, "sect", "dir", None, None)
    return jax.shard_map(shards, mesh=mesh, in_specs=in_specs, out_specs=out_specs, check_vma=False)
```

```python
import jax
import jax.numpy as jnp
from jax import lax
from jax.experimental import pallas as pl
from jax.experimental.pallas import tpu as pltpu
from jax.sharding import PartitionSpec as P

REACH = 2
MIB = 1 << 20
far_offsets = [
    (row_step, col_step)
    for row_step in range(-REACH, REACH + 1)
    for col_step in range(-REACH, REACH + 1)
    if max(abs(row_step), abs(col_step)) == REACH
]
VMEM = pl.BlockSpec(memory_space=pltpu.VMEM)
SMEM = pl.BlockSpec(memory_space=pltpu.SMEM)
ANY = pl.BlockSpec(memory_space=pl.ANY)


def params(mib=56):
    return pltpu.CompilerParams(vmem_limit_bytes=mib * MIB)


def cost(micros):
    return pl.CostEstimate(flops=int(micros * 1.15e9), bytes_accessed=int(micros * 3.69e6), transcendentals=0)


def swap_pairs(count, first):
    pairs = []
    for i in range(count):
        partner = i + 1 if (i - first) % 2 == 0 else i - 1
        pairs.append((i, partner if 0 <= partner < count else None))
    return pairs


def swap_cols(array, first):
    rows, cols = lax.axis_size("sect"), lax.axis_size("dir")
    sends = []
    for row in range(rows):
        for col, partner in swap_pairs(cols, first):
            to = (row ^ 1) * cols + col if partner is None else row * cols + partner
            sends.append((row * cols + col, to))
    return lax.ppermute(array, ("sect", "dir"), sends)


def swap_rows(array, first):
    rows, cols = lax.axis_size("sect"), lax.axis_size("dir")
    sends = []
    for row, partner in swap_pairs(rows, first):
        for col in range(cols):
            to = row * cols + (col ^ 1) if partner is None else partner * cols + col
            sends.append((row * cols + col, to))
    return lax.ppermute(array, ("sect", "dir"), sends)


def complex_dot(left_real, left_imag, right):
    rows = left_real.shape[0]
    cols = right.shape[1] // 2
    both = jnp.dot(
        jnp.concatenate([left_real, left_imag], axis=0), right, preferred_element_type=jnp.float32
    )
    real = both[:rows, :cols] - both[rows:, cols:]
    imag = both[:rows, cols:] + both[rows:, :cols]
    return real, imag


def pattern_kernel(
    live_ref, unknowns_ref, aggregate_ref, out_ref, near_ref, cross_ref, leaves_ref,
):
    rows, cols, _, narrow, sides = out_ref.shape
    deep, wide, size = unknowns_ref.shape[1:4]

    @pl.when(pl.program_id(0) == 0)
    def _():
        for u in range(deep):
            for v in range(wide):
                keep = live_ref[u, v].astype(jnp.float32).astype(jnp.bfloat16)
                at = (u * wide + v) * size
                for c in range(2):
                    leaves_ref[at : at + size, c * sides : (c + 1) * sides] = (
                        unknowns_ref[c, u, v] * keep
                    )

    left = [
        jnp.concatenate([aggregate_ref[c, u, v] for u in range(deep) for v in range(wide)], axis=1)
        for c in range(2)
    ]
    real, imag = complex_dot(left[0], left[1], leaves_ref[...])
    for row in range(rows):
        for col in range(cols):
            at = (col * rows + row) * narrow
            out_ref[row, col, 0] = real[at : at + narrow].astype(jnp.bfloat16)
            out_ref[row, col, 1] = imag[at : at + narrow].astype(jnp.bfloat16)

    @pl.when(pl.program_id(0) == 0)
    def _():
        odd = lax.rem(lax.axis_index("dir"), 2)

        def leaf(u, v, c):
            at = pl.multiple_of((u * wide + v) * size, size)
            return leaves_ref[pl.ds(at, size), c * sides : (c + 1) * sides]

        for c in range(2):
            for u in range(deep):
                near_ref[c, u] = leaf(u, 1 - odd, c)
                cross_ref[c, u] = leaf(u, odd, c)


def translate_kernel(
    from_ref, coef_ref, out_ref, held_ref, made_ref, coefs_ref, turned_ref, wide_ref, coef_sem, in_sem,
    out_sem,
):
    box_rows, box_cols, _, narrow, sides = from_ref.shape
    lanes = min(128, sides)

    def across(place):
        return pl.ds(pl.multiple_of(place * lanes, lanes), lanes)

    def arrival(place):
        return pltpu.make_async_copy(
            from_ref.at[..., across(place)], held_ref.at[..., across(place)], in_sem.at[place]
        )

    def departure(place):
        return pltpu.make_async_copy(
            made_ref.at[..., across(place)], out_ref.at[..., across(place)], out_sem.at[place]
        )

    coefs_here = pltpu.make_async_copy(coef_ref, coefs_ref, coef_sem)
    coefs_here.start()
    for place in range(sides // lanes):
        arrival(place).start()
    coefs_here.wait()
    turned_ref[...] = coefs_ref[...].T
    first = pl.multiple_of(lax.axis_index("sect") * narrow, narrow)
    coefs = turned_ref[pl.ds(first, narrow)]
    for index in range(coefs.shape[1]):
        wide_ref[index] = jnp.broadcast_to(coefs[:, index : index + 1], (narrow, lanes))

    def tile(place, carry):
        arrival(place).wait()
        for col in range(box_cols):
            totals = {}
            for source in range(box_rows):
                held = {
                    step: [
                        held_ref[source, col + step, c, :, across(place)].astype(jnp.float32)
                        for c in range(2)
                    ]
                    for step in range(-REACH, REACH + 1)
                    if 0 <= col + step < box_cols
                }
                for target in range(max(0, source - REACH), min(box_rows, source + REACH + 1)):
                    real = imag = None
                    for index, (row_step, step) in enumerate(far_offsets):
                        if row_step != source - target or step not in held:
                            continue
                        coef_real, coef_imag = wide_ref[2 * index], wide_ref[2 * index + 1]
                        from_real, from_imag = held[step]
                        term_real = coef_real * from_real - coef_imag * from_imag
                        term_imag = coef_real * from_imag + coef_imag * from_real
                        real = term_real if real is None else real + term_real
                        imag = term_imag if imag is None else imag + term_imag
                    if real is None:
                        continue
                    real = real.astype(jnp.bfloat16).astype(jnp.float32)
                    imag = imag.astype(jnp.bfloat16).astype(jnp.float32)
                    if target in totals:
                        old = totals[target]
                        real, imag = old[0] + real, old[1] + imag
                    totals[target] = (real, imag)
            for target in range(box_rows):
                for c in range(2):
                    made_ref[target, col, c, :, across(place)] = (
                        totals[target][c].astype(jnp.bfloat16)
                        if target in totals
                        else jnp.zeros((narrow, lanes), jnp.bfloat16)
                    )
        departure(place).start()
        return carry

    lax.fori_loop(0, sides // lanes, tile, 0)
    for place in range(sides // lanes):
        departure(place).wait()


def translate_grid(sources, coefs):
    box_rows, box_cols = sources.shape[:2]
    widened = jnp.pad(sources.astype(jnp.float32), ((REACH, REACH), (REACH, REACH), (0, 0), (0, 0), (0, 0)))
    accum = jnp.zeros(sources.shape, jnp.float32)
    for row_step in range(-REACH, REACH + 1):
        total = jnp.zeros(sources.shape, jnp.float32)
        for index, (step_row, step_col) in enumerate(far_offsets):
            if step_row == row_step:
                shifted = widened[
                    REACH + step_row : REACH + step_row + box_rows,
                    REACH + step_col : REACH + step_col + box_cols,
                ]
                coef_real = coefs[index, 0][None, None, :, None]
                coef_imag = coefs[index, 1][None, None, :, None]
                real = coef_real * shifted[:, :, 0] - coef_imag * shifted[:, :, 1]
                imag = coef_real * shifted[:, :, 1] + coef_imag * shifted[:, :, 0]
                total = total + jnp.stack([real, imag], axis=2)
        accum = accum + total.astype(jnp.bfloat16).astype(jnp.float32)
    return accum.astype(jnp.bfloat16)


def move(copies, sem):
    arrivals = [
        pltpu.make_async_copy(source, held, sem.at[0, i]) for i, (source, held, _) in enumerate(copies)
    ]
    departures = [
        pltpu.make_async_copy(held, target, sem.at[1, i]) for i, (_, held, target) in enumerate(copies)
    ]
    for copy in arrivals:
        copy.start()
    for arrival, departure in zip(arrivals, departures):
        arrival.wait()
        departure.start()
    for copy in departures:
        copy.wait()


def row_kernel(
    near_ref, cross_ref, from_cross_ref, from_near_ref, out_near_ref, out_cross_ref, held_ref, sem
):
    odd = lax.rem(lax.axis_index("sect"), 2)
    copies = []
    for slot, ref in enumerate((near_ref, cross_ref, from_cross_ref, from_near_ref)):
        copies.append((ref.at[:, 1 - odd], held_ref.at[0, slot], out_near_ref.at[:, slot]))
        copies.append((ref.at[:, odd], held_ref.at[1, slot], out_cross_ref.at[:, slot]))
    move(copies, sem)


def near_kernel(
    near_ref, cross_ref, from_cross_ref, from_near_ref, row_near_ref, row_cross_ref, blocks_ref,
    out_ref, grid_ref,
):
    sides = near_ref.shape[3]
    deep = near_ref.shape[1]
    wide = 2
    leaf = pl.program_id(0)

    @pl.when(leaf == 0)
    def _():
        col_at, col_count = lax.axis_index("dir"), lax.axis_size("dir")
        row_at, row_count = lax.axis_index("sect"), lax.axis_size("sect")
        col_odd, row_odd = lax.rem(col_at, 2), lax.rem(row_at, 2)
        columns = (2 - col_odd, 1 + col_odd, 3 * col_odd, 3 - 3 * col_odd)
        row_next, row_last = 3 - 3 * row_odd, 3 * row_odd
        no_col = ((col_odd == 0) & (col_at == 0)) | ((col_odd == 1) & (col_at == col_count - 1))
        no_row = ((row_odd == 0) & (row_at == 0)) | ((row_odd == 1) & (row_at == row_count - 1))
        for slot, ref in enumerate((near_ref, cross_ref, from_cross_ref, from_near_ref)):
            for c in range(2):
                half = slice(c * sides, (c + 1) * sides)
                for u in range(deep):
                    grid_ref[1 + u, columns[slot], :, half] = ref[c, u]
                grid_ref[row_next, columns[slot], :, half] = row_near_ref[c, slot]
                grid_ref[row_last, columns[slot], :, half] = row_cross_ref[c, slot]

        @pl.when(no_col)
        def _():
            for i in range(deep + 2):
                grid_ref[i, columns[2]] = jnp.zeros(grid_ref.shape[2:], grid_ref.dtype)

        @pl.when(no_row)
        def _():
            for j in range(wide + 2):
                grid_ref[row_last, j] = jnp.zeros(grid_ref.shape[2:], grid_ref.dtype)

    u, v = leaf // wide, lax.rem(leaf, wide)
    right = jnp.concatenate(
        [grid_ref[u + a, v + b] for a in range(3) for b in range(3)], axis=0
    )
    left = [jnp.concatenate([blocks_ref[c, 0, 0, k] for k in range(9)], axis=1) for c in range(2)]
    real, imag = complex_dot(left[0], left[1], right)
    out_ref[0, 0, 0] = real
    out_ref[1, 0, 0] = imag


def far_kernel(
    live_ref, incoming_ref, disaggregate_ref, near_ref, out_ref, right_ref, made_ref, in_sem, out_sem
):
    rows, cols, _, narrow, sides = incoming_ref.shape
    deep, wide = live_ref.shape

    def arrival(row, c):
        return pltpu.make_async_copy(
            incoming_ref.at[row, :, c],
            right_ref.at[:, row, :, c * sides : (c + 1) * sides],
            in_sem.at[row, c],
        )

    def departure(u, v):
        return pltpu.make_async_copy(
            made_ref.at[:, u, v], out_ref.at[:, u, v], out_sem.at[u, v]
        )

    places = [(row, c) for row in range(rows) for c in range(2)]
    for place in places:
        arrival(*place).start()
    for place in places:
        arrival(*place).wait()
    right = right_ref[...].reshape(cols * rows * narrow, 2 * sides)
    for u in range(deep):
        for v in range(wide):
            live = live_ref[u, v].astype(jnp.float32)
            real, imag = complex_dot(disaggregate_ref[0, u, v], disaggregate_ref[1, u, v], right)
            made_ref[0, u, v] = (near_ref[0, u, v] + real) * live
            made_ref[1, u, v] = (near_ref[1, u, v] + imag) * live
            departure(u, v).start()
    for u in range(deep):
        for v in range(wide):
            departure(u, v).wait()


def shards(unknowns, leaf_live, near_blocks, aggregate, disaggregate, translate):
    sect_count, dir_count = lax.axis_size("sect"), lax.axis_size("dir")
    _, deep, wide, size, sides = unknowns.shape
    total_dirs = aggregate.shape[3]
    narrow = total_dirs // (sect_count * dir_count)
    held = translate.shape[2]
    bf16, f32 = jnp.bfloat16, jnp.float32
    tiled = narrow % 16 == 0
    steps = 2
    rows, cols = (sect_count, dir_count) if tiled else (1, steps)
    block = total_dirs // (rows * cols)

    column = jax.ShapeDtypeStruct((2, deep, size, sides), bf16)
    whole = [pl.BlockSpec(a.shape, lambda i, n=len(a.shape): (0,) * n) for a in (unknowns, column)]
    patterns, col_near, col_cross = pl.pallas_call(
        pattern_kernel,
        grid=(steps,),
        in_specs=[
            SMEM,
            whole[0],
            pl.BlockSpec((2, deep, wide, total_dirs // steps, size), lambda i: (0, 0, 0, i, 0)),
        ],
        out_specs=[
            pl.BlockSpec((rows, cols // steps, 2, block, sides), lambda i: (0, i, 0, 0, 0)),
            whole[1],
            whole[1],
        ],
        out_shape=[jax.ShapeDtypeStruct((rows, cols, 2, block, sides), bf16), column, column],
        scratch_shapes=[pltpu.VMEM((deep * wide * size, 2 * sides), bf16)],
        compiler_params=params(),
        name="patterns",
    )(leaf_live, unknowns, aggregate)
    from_cross = swap_cols(col_cross, 1)
    from_near = swap_cols(col_near, 0)

    row = jax.ShapeDtypeStruct((2, 4, size, sides), bf16)
    row_near, row_cross = pl.pallas_call(
        row_kernel,
        in_specs=[ANY] * 4,
        out_specs=[ANY] * 2,
        out_shape=[row, row],
        scratch_shapes=[
            pltpu.VMEM((2, 4, 2, size, sides), bf16),
            pltpu.SemaphoreType.DMA((2, 8)),
        ],
        compiler_params=params(),
        cost_estimate=cost(4000),
        name="rows",
    )(col_near, col_cross, from_cross, from_near)

    def spread(array):
        flat = array.reshape(rows * cols, 2, block, sides)
        return lax.all_to_all(flat, ("sect", "dir"), split_axis=0, concat_axis=0, tiled=True).reshape(array.shape)

    if tiled:
        own = spread(patterns)
        own, _, _ = lax.optimization_barrier((own, row_near, row_cross))
        lanes = min(128, sides)
        incoming = pl.pallas_call(
            translate_kernel,
            in_specs=[ANY] * 2,
            out_specs=ANY,
            out_shape=jax.ShapeDtypeStruct(own.shape, bf16),
            scratch_shapes=[
                pltpu.VMEM(own.shape, bf16),
                pltpu.VMEM(own.shape, bf16),
                pltpu.VMEM((2 * len(far_offsets), held), f32),
                pltpu.VMEM((held, 2 * len(far_offsets)), f32),
                pltpu.VMEM((2 * len(far_offsets), narrow, lanes), f32),
                pltpu.SemaphoreType.DMA,
                pltpu.SemaphoreType.DMA((sides // lanes,)),
                pltpu.SemaphoreType.DMA((sides // lanes,)),
            ],
            compiler_params=params(16),
            cost_estimate=cost(4000),
            name="translations",
        )(own, translate.reshape(2 * len(far_offsets), held))
        returned = spread(incoming)
    else:
        split = (2, dir_count, sect_count, narrow, sides)
        base = patterns[0].transpose(1, 0, 2, 3).reshape(split).transpose(0, 2, 1, 3, 4)
        base = base.reshape(2, total_dirs, sides)[None, None]
        own = lax.all_to_all(base, "sect", split_axis=3, concat_axis=0, tiled=True)
        own = lax.all_to_all(own, "dir", split_axis=3, concat_axis=1, tiled=True)
        coefs = lax.dynamic_slice_in_dim(translate, lax.axis_index("sect") * narrow, narrow, 2)
        incoming = translate_grid(own, coefs)
        returned = lax.all_to_all(incoming, "sect", split_axis=0, concat_axis=3, tiled=True)
        returned = lax.all_to_all(returned, "dir", split_axis=1, concat_axis=3, tiled=True)[0, 0]
        returned = returned.reshape(2, cols, block, sides).transpose(1, 0, 2, 3)[None]

    row_near = swap_rows(row_near, 0)
    row_cross = swap_rows(row_cross, 1)
    field = jax.ShapeDtypeStruct(unknowns.shape, f32)
    near = pl.pallas_call(
        near_kernel,
        grid=(deep * wide,),
        in_specs=[VMEM] * 6
        + [pl.BlockSpec((2, 1, 1, 9, size, size), lambda i: (0, i // wide, i % wide, 0, 0, 0))],
        out_specs=pl.BlockSpec((2, 1, 1, size, sides), lambda i: (0, i // wide, i % wide, 0, 0)),
        out_shape=field,
        scratch_shapes=[pltpu.VMEM((deep + 2, wide + 2, size, 2 * sides), bf16)],
        compiler_params=params(16),
        cost_estimate=cost(4000),
        name="near",
    )(col_near, col_cross, from_cross, from_near, row_near, row_cross, near_blocks)
    return pl.pallas_call(
        far_kernel,
        in_specs=[SMEM, ANY, VMEM, VMEM],
        out_specs=ANY,
        out_shape=field,
        scratch_shapes=[
            pltpu.VMEM((cols, rows, block, 2 * sides), bf16),
            pltpu.VMEM(unknowns.shape, f32),
            pltpu.SemaphoreType.DMA((rows, 2)),
            pltpu.SemaphoreType.DMA((deep, wide)),
        ],
        compiler_params=params(16),
        name="far",
    )(leaf_live, returned, disaggregate, near)


def solution(mesh):
    in_specs = (
        P(None, "sect", "dir", None, None),
        P("sect", "dir"),
        P(None, "sect", "dir", None, None, None),
        P(None, "sect", "dir", None, None),
        P(None, "sect", "dir", None, None),
        P(None, None, "dir"),
    )
    out_specs = P(None, "sect", "dir", None, None)
    return jax.shard_map(shards, mesh=mesh, in_specs=in_specs, out_specs=out_specs, check_vma=False)
```

```python
import jax
import jax.numpy as jnp
from jax import lax
from jax.experimental import pallas as pl
from jax.experimental.pallas import tpu as pltpu
from jax.sharding import PartitionSpec as P

REACH = 2
MIB = 1 << 20
far_offsets = [
    (row_step, col_step)
    for row_step in range(-REACH, REACH + 1)
    for col_step in range(-REACH, REACH + 1)
    if max(abs(row_step), abs(col_step)) == REACH
]
VMEM = pl.BlockSpec(memory_space=pltpu.VMEM)
ANY = pl.BlockSpec(memory_space=pl.ANY)


def params(mib=56):
    return pltpu.CompilerParams(vmem_limit_bytes=mib * MIB)


def cost(micros):
    return pl.CostEstimate(flops=int(micros * 1.15e9), bytes_accessed=int(micros * 3.69e6), transcendentals=0)


def swap_pairs(count, first):
    pairs = []
    for i in range(count):
        partner = i + 1 if (i - first) % 2 == 0 else i - 1
        pairs.append((i, partner if 0 <= partner < count else None))
    return pairs


def swap_cols(array, first):
    rows, cols = lax.axis_size("sect"), lax.axis_size("dir")
    sends = []
    for row in range(rows):
        for col, partner in swap_pairs(cols, first):
            to = (row ^ 1) * cols + col if partner is None else row * cols + partner
            sends.append((row * cols + col, to))
    return lax.ppermute(array, ("sect", "dir"), sends)


def swap_rows(array, first, turn=0):
    rows, cols = lax.axis_size("sect"), lax.axis_size("dir")
    sends = []
    for row, partner in swap_pairs(rows, first):
        for col in range(cols):
            to = row * cols + (col ^ 1) if partner is None else partner * cols + (col ^ turn)
            sends.append((row * cols + col, to))
    return lax.ppermute(array, ("sect", "dir"), sends)


def complex_dot(left_real, left_imag, right):
    rows = left_real.shape[0]
    cols = right.shape[1] // 2
    both = jnp.dot(
        jnp.concatenate([left_real, left_imag], axis=0), right, preferred_element_type=jnp.float32
    )
    real = both[:rows, :cols] - both[rows:, cols:]
    imag = both[:rows, cols:] + both[rows:, :cols]
    return real, imag


def pattern_kernel(
    live_ref, unknowns_ref, aggregate_ref, out_ref, near_ref, cross_ref, corner_near_ref,
    corner_cross_ref, leaves_ref,
):
    rows, cols, _, narrow, sides = out_ref.shape
    deep, wide, size = unknowns_ref.shape[1:4]

    @pl.when(pl.program_id(0) == 0)
    def _():
        for u in range(deep):
            for v in range(wide):
                keep = live_ref[u, v].astype(jnp.float32).astype(jnp.bfloat16)
                at = (u * wide + v) * size
                for c in range(2):
                    leaves_ref[at : at + size, c * sides : (c + 1) * sides] = (
                        unknowns_ref[c, u, v] * keep
                    )

    left = [
        jnp.concatenate([aggregate_ref[c, u, v] for u in range(deep) for v in range(wide)], axis=1)
        for c in range(2)
    ]
    real, imag = complex_dot(left[0], left[1], leaves_ref[...])
    for row in range(rows):
        for col in range(cols):
            at = (col * rows + row) * narrow
            out_ref[row, col, 0] = real[at : at + narrow].astype(jnp.bfloat16)
            out_ref[row, col, 1] = imag[at : at + narrow].astype(jnp.bfloat16)

    @pl.when(pl.program_id(0) == 0)
    def _():
        odd = lax.rem(lax.axis_index("dir"), 2)
        row_odd = lax.rem(lax.axis_index("sect"), 2)

        def leaf(u, v, c):
            at = pl.multiple_of((u * wide + v) * size, size)
            return leaves_ref[pl.ds(at, size), c * sides : (c + 1) * sides]

        for c in range(2):
            for u in range(deep):
                near_ref[c, u] = leaf(u, 1 - odd, c)
                cross_ref[c, u] = leaf(u, odd, c)
            corner_near_ref[c] = leaf(1 - row_odd, 1 - odd, c)
            corner_cross_ref[c] = leaf(row_odd, 1 - odd, c)


def translate_kernel(
    from_ref, coef_ref, out_ref, held_ref, made_ref, coefs_ref, turned_ref, wide_ref, coef_sem, in_sem,
    out_sem,
):
    box_rows, box_cols, _, narrow, sides = from_ref.shape
    lanes = min(128, sides)

    def across(place):
        return pl.ds(pl.multiple_of(place * lanes, lanes), lanes)

    def arrival(place):
        return pltpu.make_async_copy(
            from_ref.at[..., across(place)], held_ref.at[..., across(place)], in_sem.at[place]
        )

    def departure(place):
        return pltpu.make_async_copy(
            made_ref.at[..., across(place)], out_ref.at[..., across(place)], out_sem.at[place]
        )

    coefs_here = pltpu.make_async_copy(coef_ref, coefs_ref, coef_sem)
    coefs_here.start()
    for place in range(sides // lanes):
        arrival(place).start()
    coefs_here.wait()
    turned_ref[...] = coefs_ref[...].T
    first = pl.multiple_of(lax.axis_index("sect") * narrow, narrow)
    coefs = turned_ref[pl.ds(first, narrow)]
    for index in range(coefs.shape[1]):
        wide_ref[index] = jnp.broadcast_to(coefs[:, index : index + 1], (narrow, lanes))

    def tile(place, carry):
        arrival(place).wait()
        for col in range(box_cols):
            totals = {}
            for source in range(box_rows):
                held = {
                    step: [
                        held_ref[source, col + step, c, :, across(place)].astype(jnp.float32)
                        for c in range(2)
                    ]
                    for step in range(-REACH, REACH + 1)
                    if 0 <= col + step < box_cols
                }
                for target in range(max(0, source - REACH), min(box_rows, source + REACH + 1)):
                    real = imag = None
                    for index, (row_step, step) in enumerate(far_offsets):
                        if row_step != source - target or step not in held:
                            continue
                        coef_real, coef_imag = wide_ref[2 * index], wide_ref[2 * index + 1]
                        from_real, from_imag = held[step]
                        term_real = coef_real * from_real - coef_imag * from_imag
                        term_imag = coef_real * from_imag + coef_imag * from_real
                        real = term_real if real is None else real + term_real
                        imag = term_imag if imag is None else imag + term_imag
                    if real is None:
                        continue
                    real = real.astype(jnp.bfloat16).astype(jnp.float32)
                    imag = imag.astype(jnp.bfloat16).astype(jnp.float32)
                    if target in totals:
                        old = totals[target]
                        real, imag = old[0] + real, old[1] + imag
                    totals[target] = (real, imag)
            for target in range(box_rows):
                for c in range(2):
                    made_ref[target, col, c, :, across(place)] = (
                        totals[target][c].astype(jnp.bfloat16)
                        if target in totals
                        else jnp.zeros((narrow, lanes), jnp.bfloat16)
                    )
        departure(place).start()
        return carry

    lax.fori_loop(0, sides // lanes, tile, 0)
    for place in range(sides // lanes):
        departure(place).wait()


def translate_grid(sources, coefs):
    box_rows, box_cols = sources.shape[:2]
    widened = jnp.pad(sources.astype(jnp.float32), ((REACH, REACH), (REACH, REACH), (0, 0), (0, 0), (0, 0)))
    accum = jnp.zeros(sources.shape, jnp.float32)
    for row_step in range(-REACH, REACH + 1):
        total = jnp.zeros(sources.shape, jnp.float32)
        for index, (step_row, step_col) in enumerate(far_offsets):
            if step_row == row_step:
                shifted = widened[
                    REACH + step_row : REACH + step_row + box_rows,
                    REACH + step_col : REACH + step_col + box_cols,
                ]
                coef_real = coefs[index, 0][None, None, :, None]
                coef_imag = coefs[index, 1][None, None, :, None]
                real = coef_real * shifted[:, :, 0] - coef_imag * shifted[:, :, 1]
                imag = coef_real * shifted[:, :, 1] + coef_imag * shifted[:, :, 0]
                total = total + jnp.stack([real, imag], axis=2)
        accum = accum + total.astype(jnp.bfloat16).astype(jnp.float32)
    return accum.astype(jnp.bfloat16)


def move(copies, sem):
    arrivals = [
        pltpu.make_async_copy(source, held, sem.at[0, i]) for i, (source, held, _) in enumerate(copies)
    ]
    departures = [
        pltpu.make_async_copy(held, target, sem.at[1, i]) for i, (_, held, target) in enumerate(copies)
    ]
    for copy in arrivals:
        copy.start()
    for arrival, departure in zip(arrivals, departures):
        arrival.wait()
        departure.start()
    for copy in departures:
        copy.wait()


def row_kernel(near_ref, cross_ref, from_cross_ref, out_near_ref, out_cross_ref, held_ref, sem):
    odd = lax.rem(lax.axis_index("sect"), 2)
    copies = []
    for slot, ref in enumerate((near_ref, cross_ref, from_cross_ref)):
        copies.append((ref.at[:, 1 - odd], held_ref.at[0, slot], out_near_ref.at[:, slot]))
        copies.append((ref.at[:, odd], held_ref.at[1, slot], out_cross_ref.at[:, slot]))
    move(copies, sem)


def near_kernel(
    near_ref, cross_ref, from_cross_ref, from_near_ref, row_near_ref, row_cross_ref, corner_near_ref,
    corner_cross_ref, blocks_ref, out_ref, grid_ref,
):
    sides = near_ref.shape[3]
    deep = near_ref.shape[1]
    wide = 2
    leaf = pl.program_id(0)

    @pl.when(leaf == 0)
    def _():
        col_at, col_count = lax.axis_index("dir"), lax.axis_size("dir")
        row_at, row_count = lax.axis_index("sect"), lax.axis_size("sect")
        col_odd, row_odd = lax.rem(col_at, 2), lax.rem(row_at, 2)
        columns = (2 - col_odd, 1 + col_odd, 3 * col_odd, 3 - 3 * col_odd)
        row_next, row_last = 3 - 3 * row_odd, 3 * row_odd
        no_col = ((col_odd == 0) & (col_at == 0)) | ((col_odd == 1) & (col_at == col_count - 1))
        no_row = ((row_odd == 0) & (row_at == 0)) | ((row_odd == 1) & (row_at == row_count - 1))
        for slot, ref in enumerate((near_ref, cross_ref, from_cross_ref, from_near_ref)):
            for c in range(2):
                half = slice(c * sides, (c + 1) * sides)
                for u in range(deep):
                    grid_ref[1 + u, columns[slot], :, half] = ref[c, u]
                if slot < 3:
                    grid_ref[row_next, columns[slot], :, half] = row_near_ref[c, slot]
                    grid_ref[row_last, columns[slot], :, half] = row_cross_ref[c, slot]
                else:
                    grid_ref[row_next, columns[slot], :, half] = corner_near_ref[c]
                    grid_ref[row_last, columns[slot], :, half] = corner_cross_ref[c]

        @pl.when(no_col)
        def _():
            for i in range(deep + 2):
                grid_ref[i, columns[2]] = jnp.zeros(grid_ref.shape[2:], grid_ref.dtype)

        @pl.when(no_row)
        def _():
            for j in range(wide + 2):
                grid_ref[row_last, j] = jnp.zeros(grid_ref.shape[2:], grid_ref.dtype)

    u, v = leaf // wide, lax.rem(leaf, wide)
    right = jnp.concatenate(
        [grid_ref[u + a, v + b] for a in range(3) for b in range(3)], axis=0
    )
    left = [jnp.concatenate([blocks_ref[c, 0, 0, k] for k in range(9)], axis=1) for c in range(2)]
    real, imag = complex_dot(left[0], left[1], right)
    out_ref[0, 0, 0] = real
    out_ref[1, 0, 0] = imag


def far_kernel(
    live_ref, incoming_ref, disaggregate_ref, near_ref, out_ref, live_here, right_ref, made_ref, live_sem,
    in_sem, out_sem,
):
    rows, cols, _, narrow, sides = incoming_ref.shape
    deep, wide = live_ref.shape

    def arrival(row, c):
        return pltpu.make_async_copy(
            incoming_ref.at[row, :, c],
            right_ref.at[:, row, :, c * sides : (c + 1) * sides],
            in_sem.at[row, c],
        )

    def departure(u, v):
        return pltpu.make_async_copy(
            made_ref.at[:, u, v], out_ref.at[:, u, v], out_sem.at[u, v]
        )

    places = [(row, c) for row in range(rows) for c in range(2)]
    live_copy = pltpu.make_async_copy(live_ref, live_here, live_sem)
    live_copy.start()
    for place in places:
        arrival(*place).start()
    live_copy.wait()
    for place in places:
        arrival(*place).wait()
    right = right_ref[...].reshape(cols * rows * narrow, 2 * sides)
    for u in range(deep):
        for v in range(wide):
            live = live_here[u : u + 1, v : v + 1].astype(jnp.float32)
            real, imag = complex_dot(disaggregate_ref[0, u, v], disaggregate_ref[1, u, v], right)
            made_ref[0, u, v] = (near_ref[0, u, v] + real) * live
            made_ref[1, u, v] = (near_ref[1, u, v] + imag) * live
            departure(u, v).start()
    for u in range(deep):
        for v in range(wide):
            departure(u, v).wait()


def shards(unknowns, leaf_live, near_blocks, aggregate, disaggregate, translate):
    sect_count, dir_count = lax.axis_size("sect"), lax.axis_size("dir")
    _, deep, wide, size, sides = unknowns.shape
    total_dirs = aggregate.shape[3]
    narrow = total_dirs // (sect_count * dir_count)
    held = translate.shape[2]
    bf16, f32 = jnp.bfloat16, jnp.float32
    tiled = narrow % 16 == 0
    steps = 1
    rows, cols = (sect_count, dir_count) if tiled else (1, steps)
    block = total_dirs // (rows * cols)

    column = jax.ShapeDtypeStruct((2, deep, size, sides), bf16)
    corner = jax.ShapeDtypeStruct((2, size, sides), bf16)
    blocks = jax.ShapeDtypeStruct((rows, cols, 2, block, sides), bf16)
    whole = [
        pl.BlockSpec(a.shape, lambda i, n=len(a.shape): (0,) * n) for a in (unknowns, column, corner)
    ]
    patterns, col_near, col_cross, corner_near, corner_cross = pl.pallas_call(
        pattern_kernel,
        grid=(steps,),
        in_specs=[
            pl.BlockSpec(memory_space=pltpu.SMEM),
            whole[0],
            pl.BlockSpec((2, deep, wide, total_dirs // steps, size), lambda i: (0, 0, 0, i, 0)),
        ],
        out_specs=[
            pl.BlockSpec((rows, cols // steps, 2, block, sides), lambda i: (0, i, 0, 0, 0)),
            whole[1],
            whole[1],
            whole[2],
            whole[2],
        ],
        out_shape=[blocks, column, column, corner, corner],
        scratch_shapes=[pltpu.VMEM((deep * wide * size, 2 * sides), bf16)],
        compiler_params=params(),
        name="patterns",
    )(leaf_live, unknowns, aggregate)
    from_cross = swap_cols(col_cross, 1)
    from_near = swap_cols(col_near, 0)
    corner_near = swap_rows(corner_near, 0, 1)
    corner_cross = swap_rows(corner_cross, 1, 1)

    row = jax.ShapeDtypeStruct((2, 3, size, sides), bf16)
    row_near, row_cross = pl.pallas_call(
        row_kernel,
        in_specs=[ANY] * 3,
        out_specs=[ANY] * 2,
        out_shape=[row, row],
        scratch_shapes=[
            pltpu.VMEM((2, 3, 2, size, sides), bf16),
            pltpu.SemaphoreType.DMA((2, 6)),
        ],
        compiler_params=params(),
        cost_estimate=cost(4000),
        name="rows",
    )(col_near, col_cross, from_cross)

    def spread(array):
        flat = array.reshape(rows * cols, 2, block, sides)
        return lax.all_to_all(flat, ("sect", "dir"), split_axis=0, concat_axis=0, tiled=True).reshape(array.shape)

    if tiled:
        own = spread(patterns)
        own, _, _ = lax.optimization_barrier((own, row_near, row_cross))
        lanes = min(128, sides)
        incoming = pl.pallas_call(
            translate_kernel,
            in_specs=[ANY] * 2,
            out_specs=ANY,
            out_shape=jax.ShapeDtypeStruct(own.shape, bf16),
            scratch_shapes=[
                pltpu.VMEM(own.shape, bf16),
                pltpu.VMEM(own.shape, bf16),
                pltpu.VMEM((2 * len(far_offsets), held), f32),
                pltpu.VMEM((held, 2 * len(far_offsets)), f32),
                pltpu.VMEM((2 * len(far_offsets), narrow, lanes), f32),
                pltpu.SemaphoreType.DMA,
                pltpu.SemaphoreType.DMA((sides // lanes,)),
                pltpu.SemaphoreType.DMA((sides // lanes,)),
            ],
            compiler_params=params(16),
            cost_estimate=cost(8),
            name="translations",
        )(own, translate.reshape(2 * len(far_offsets), held))
        returned = spread(incoming)
    else:
        split = (2, dir_count, sect_count, narrow, sides)
        base = patterns[0].transpose(1, 0, 2, 3).reshape(split).transpose(0, 2, 1, 3, 4)
        base = base.reshape(2, total_dirs, sides)[None, None]
        own = lax.all_to_all(base, "sect", split_axis=3, concat_axis=0, tiled=True)
        own = lax.all_to_all(own, "dir", split_axis=3, concat_axis=1, tiled=True)
        coefs = lax.dynamic_slice_in_dim(translate, lax.axis_index("sect") * narrow, narrow, 2)
        incoming = translate_grid(own, coefs)
        returned = lax.all_to_all(incoming, "sect", split_axis=0, concat_axis=3, tiled=True)
        returned = lax.all_to_all(returned, "dir", split_axis=1, concat_axis=3, tiled=True)[0, 0]
        returned = returned.reshape(2, cols, block, sides).transpose(1, 0, 2, 3)[None]

    row_near = swap_rows(row_near, 0)
    row_cross = swap_rows(row_cross, 1)
    field = jax.ShapeDtypeStruct(unknowns.shape, f32)
    near = pl.pallas_call(
        near_kernel,
        grid=(deep * wide,),
        in_specs=[VMEM] * 8
        + [pl.BlockSpec((2, 1, 1, 9, size, size), lambda i: (0, i // wide, i % wide, 0, 0, 0))],
        out_specs=pl.BlockSpec((2, 1, 1, size, sides), lambda i: (0, i // wide, i % wide, 0, 0)),
        out_shape=field,
        scratch_shapes=[pltpu.VMEM((deep + 2, wide + 2, size, 2 * sides), bf16)],
        compiler_params=params(16),
        cost_estimate=cost(4000),
        name="near",
    )(
        col_near, col_cross, from_cross, from_near, row_near, row_cross, corner_near, corner_cross,
        near_blocks,
    )
    return pl.pallas_call(
        far_kernel,
        in_specs=[ANY, ANY, VMEM, VMEM],
        out_specs=ANY,
        out_shape=field,
        scratch_shapes=[
            pltpu.VMEM(leaf_live.shape, jnp.int32),
            pltpu.VMEM((cols, rows, block, 2 * sides), bf16),
            pltpu.VMEM(unknowns.shape, f32),
            pltpu.SemaphoreType.DMA,
            pltpu.SemaphoreType.DMA((rows, 2)),
            pltpu.SemaphoreType.DMA((deep, wide)),
        ],
        compiler_params=params(16),
        name="far",
    )(leaf_live, returned, disaggregate, near)


def solution(mesh):
    in_specs = (
        P(None, "sect", "dir", None, None),
        P("sect", "dir"),
        P(None, "sect", "dir", None, None, None),
        P(None, "sect", "dir", None, None),
        P(None, "sect", "dir", None, None),
        P(None, None, "dir"),
    )
    out_specs = P(None, "sect", "dir", None, None)
    return jax.shard_map(shards, mesh=mesh, in_specs=in_specs, out_specs=out_specs, check_vma=False)
```

```python
import jax
import jax.numpy as jnp
from jax import lax
from jax.experimental import pallas as pl
from jax.experimental.pallas import tpu as pltpu
from jax.sharding import PartitionSpec as P

REACH = 2
MIB = 1 << 20
far_offsets = [
    (row_step, col_step)
    for row_step in range(-REACH, REACH + 1)
    for col_step in range(-REACH, REACH + 1)
    if max(abs(row_step), abs(col_step)) == REACH
]
VMEM = pl.BlockSpec(memory_space=pltpu.VMEM)
ANY = pl.BlockSpec(memory_space=pl.ANY)


def params(mib=56):
    return pltpu.CompilerParams(vmem_limit_bytes=mib * MIB)


def cost(micros):
    return pl.CostEstimate(flops=int(micros * 1.15e9), bytes_accessed=int(micros * 3.69e6), transcendentals=0)


def swap_pairs(count, first):
    pairs = []
    for i in range(count):
        partner = i + 1 if (i - first) % 2 == 0 else i - 1
        pairs.append((i, partner if 0 <= partner < count else None))
    return pairs


def swap_cols(array, first):
    rows, cols = lax.axis_size("sect"), lax.axis_size("dir")
    sends = []
    for row in range(rows):
        for col, partner in swap_pairs(cols, first):
            to = (row ^ 1) * cols + col if partner is None else row * cols + partner
            sends.append((row * cols + col, to))
    return lax.ppermute(array, ("sect", "dir"), sends)


def swap_rows(array, first, turn=0):
    rows, cols = lax.axis_size("sect"), lax.axis_size("dir")
    sends = []
    for row, partner in swap_pairs(rows, first):
        for col in range(cols):
            to = row * cols + (col ^ 1) if partner is None else partner * cols + (col ^ turn)
            sends.append((row * cols + col, to))
    return lax.ppermute(array, ("sect", "dir"), sends)


def complex_dot(left_real, left_imag, right):
    rows = left_real.shape[0]
    cols = right.shape[1] // 2
    both = jnp.dot(
        jnp.concatenate([left_real, left_imag], axis=0), right, preferred_element_type=jnp.float32
    )
    real = both[:rows, :cols] - both[rows:, cols:]
    imag = both[:rows, cols:] + both[rows:, :cols]
    return real, imag


def pattern_kernel(
    live_ref, unknowns_ref, aggregate_ref, out_ref, near_ref, cross_ref, corner_near_ref,
    corner_cross_ref, leaves_ref,
):
    rows, cols, _, narrow, sides = out_ref.shape
    deep, wide, size = unknowns_ref.shape[1:4]

    @pl.when(pl.program_id(0) == 0)
    def _():
        for u in range(deep):
            for v in range(wide):
                keep = live_ref[u, v].astype(jnp.float32).astype(jnp.bfloat16)
                at = (u * wide + v) * size
                for c in range(2):
                    leaves_ref[at : at + size, c * sides : (c + 1) * sides] = (
                        unknowns_ref[c, u, v] * keep
                    )

    left = [
        jnp.concatenate([aggregate_ref[c, u, v] for u in range(deep) for v in range(wide)], axis=1)
        for c in range(2)
    ]
    real, imag = complex_dot(left[0], left[1], leaves_ref[...])
    for row in range(rows):
        for col in range(cols):
            at = (col * rows + row) * narrow
            out_ref[row, col, 0] = real[at : at + narrow].astype(jnp.bfloat16)
            out_ref[row, col, 1] = imag[at : at + narrow].astype(jnp.bfloat16)

    @pl.when(pl.program_id(0) == 0)
    def _():
        odd = lax.rem(lax.axis_index("dir"), 2)
        row_odd = lax.rem(lax.axis_index("sect"), 2)

        def leaf(u, v, c):
            at = pl.multiple_of((u * wide + v) * size, size)
            return leaves_ref[pl.ds(at, size), c * sides : (c + 1) * sides]

        for c in range(2):
            for u in range(deep):
                near_ref[c, u] = leaf(u, 1 - odd, c)
                cross_ref[c, u] = leaf(u, odd, c)
            corner_near_ref[c] = leaf(1 - row_odd, 1 - odd, c)
            corner_cross_ref[c] = leaf(row_odd, 1 - odd, c)


def translate_kernel(from_ref, coef_ref, out_ref, turned_ref, wide_ref):
    box_rows, box_cols, _, narrow, sides = from_ref.shape
    lanes = min(128, sides)

    def across(place):
        return pl.ds(pl.multiple_of(place * lanes, lanes), lanes)

    turned_ref[...] = coef_ref[...].T
    first = pl.multiple_of(lax.axis_index("sect") * narrow, narrow)
    coefs = turned_ref[pl.ds(first, narrow)]
    for index in range(coefs.shape[1]):
        wide_ref[index] = jnp.broadcast_to(coefs[:, index : index + 1], (narrow, lanes))

    def tile(place, carry):
        for col in range(box_cols):
            totals = {}
            for source in range(box_rows):
                held = {
                    step: [
                        from_ref[source, col + step, c, :, across(place)].astype(jnp.float32)
                        for c in range(2)
                    ]
                    for step in range(-REACH, REACH + 1)
                    if 0 <= col + step < box_cols
                }
                for target in range(max(0, source - REACH), min(box_rows, source + REACH + 1)):
                    real = imag = None
                    for index, (row_step, step) in enumerate(far_offsets):
                        if row_step != source - target or step not in held:
                            continue
                        coef_real, coef_imag = wide_ref[2 * index], wide_ref[2 * index + 1]
                        from_real, from_imag = held[step]
                        term_real = coef_real * from_real - coef_imag * from_imag
                        term_imag = coef_real * from_imag + coef_imag * from_real
                        real = term_real if real is None else real + term_real
                        imag = term_imag if imag is None else imag + term_imag
                    if real is None:
                        continue
                    real = real.astype(jnp.bfloat16).astype(jnp.float32)
                    imag = imag.astype(jnp.bfloat16).astype(jnp.float32)
                    if target in totals:
                        old = totals[target]
                        real, imag = old[0] + real, old[1] + imag
                    totals[target] = (real, imag)
            for target in range(box_rows):
                for c in range(2):
                    out_ref[target, col, c, :, across(place)] = (
                        totals[target][c].astype(jnp.bfloat16)
                        if target in totals
                        else jnp.zeros((narrow, lanes), jnp.bfloat16)
                    )
        return carry

    lax.fori_loop(0, sides // lanes, tile, 0)


def translate_grid(sources, coefs):
    box_rows, box_cols = sources.shape[:2]
    widened = jnp.pad(sources.astype(jnp.float32), ((REACH, REACH), (REACH, REACH), (0, 0), (0, 0), (0, 0)))
    accum = jnp.zeros(sources.shape, jnp.float32)
    for row_step in range(-REACH, REACH + 1):
        total = jnp.zeros(sources.shape, jnp.float32)
        for index, (step_row, step_col) in enumerate(far_offsets):
            if step_row == row_step:
                shifted = widened[
                    REACH + step_row : REACH + step_row + box_rows,
                    REACH + step_col : REACH + step_col + box_cols,
                ]
                coef_real = coefs[index, 0][None, None, :, None]
                coef_imag = coefs[index, 1][None, None, :, None]
                real = coef_real * shifted[:, :, 0] - coef_imag * shifted[:, :, 1]
                imag = coef_real * shifted[:, :, 1] + coef_imag * shifted[:, :, 0]
                total = total + jnp.stack([real, imag], axis=2)
        accum = accum + total.astype(jnp.bfloat16).astype(jnp.float32)
    return accum.astype(jnp.bfloat16)


def move(copies, sem):
    arrivals = [
        pltpu.make_async_copy(source, held, sem.at[0, i]) for i, (source, held, _) in enumerate(copies)
    ]
    departures = [
        pltpu.make_async_copy(held, target, sem.at[1, i]) for i, (_, held, target) in enumerate(copies)
    ]
    for copy in arrivals:
        copy.start()
    for arrival, departure in zip(arrivals, departures):
        arrival.wait()
        departure.start()
    for copy in departures:
        copy.wait()


def row_kernel(near_ref, cross_ref, from_cross_ref, out_near_ref, out_cross_ref, held_ref, sem):
    odd = lax.rem(lax.axis_index("sect"), 2)
    copies = []
    for slot, ref in enumerate((near_ref, cross_ref, from_cross_ref)):
        copies.append((ref.at[:, 1 - odd], held_ref.at[0, slot], out_near_ref.at[:, slot]))
        copies.append((ref.at[:, odd], held_ref.at[1, slot], out_cross_ref.at[:, slot]))
    move(copies, sem)


def near_kernel(
    near_ref, cross_ref, from_cross_ref, from_near_ref, row_near_ref, row_cross_ref, corner_near_ref,
    corner_cross_ref, blocks_ref, out_ref, grid_ref,
):
    sides = near_ref.shape[3]
    deep = near_ref.shape[1]
    wide = 2
    leaf = pl.program_id(0)

    @pl.when(leaf == 0)
    def _():
        col_at, col_count = lax.axis_index("dir"), lax.axis_size("dir")
        row_at, row_count = lax.axis_index("sect"), lax.axis_size("sect")
        col_odd, row_odd = lax.rem(col_at, 2), lax.rem(row_at, 2)
        columns = (2 - col_odd, 1 + col_odd, 3 * col_odd, 3 - 3 * col_odd)
        row_next, row_last = 3 - 3 * row_odd, 3 * row_odd
        no_col = ((col_odd == 0) & (col_at == 0)) | ((col_odd == 1) & (col_at == col_count - 1))
        no_row = ((row_odd == 0) & (row_at == 0)) | ((row_odd == 1) & (row_at == row_count - 1))
        for slot, ref in enumerate((near_ref, cross_ref, from_cross_ref, from_near_ref)):
            for c in range(2):
                half = slice(c * sides, (c + 1) * sides)
                for u in range(deep):
                    grid_ref[1 + u, columns[slot], :, half] = ref[c, u]
                if slot < 3:
                    grid_ref[row_next, columns[slot], :, half] = row_near_ref[c, slot]
                    grid_ref[row_last, columns[slot], :, half] = row_cross_ref[c, slot]
                else:
                    grid_ref[row_next, columns[slot], :, half] = corner_near_ref[c]
                    grid_ref[row_last, columns[slot], :, half] = corner_cross_ref[c]

        @pl.when(no_col)
        def _():
            for i in range(deep + 2):
                grid_ref[i, columns[2]] = jnp.zeros(grid_ref.shape[2:], grid_ref.dtype)

        @pl.when(no_row)
        def _():
            for j in range(wide + 2):
                grid_ref[row_last, j] = jnp.zeros(grid_ref.shape[2:], grid_ref.dtype)

    u, v = leaf // wide, lax.rem(leaf, wide)
    right = jnp.concatenate(
        [grid_ref[u + a, v + b] for a in range(3) for b in range(3)], axis=0
    )
    left = [jnp.concatenate([blocks_ref[c, 0, 0, k] for k in range(9)], axis=1) for c in range(2)]
    real, imag = complex_dot(left[0], left[1], right)
    out_ref[0, 0, 0] = real
    out_ref[1, 0, 0] = imag


def far_kernel(
    live_ref, incoming_ref, disaggregate_ref, near_ref, out_ref, live_here, right_ref, made_ref, live_sem,
    in_sem, out_sem,
):
    rows, cols, _, narrow, sides = incoming_ref.shape
    deep, wide = live_ref.shape

    def arrival(row, c):
        return pltpu.make_async_copy(
            incoming_ref.at[row, :, c],
            right_ref.at[:, row, :, c * sides : (c + 1) * sides],
            in_sem.at[row, c],
        )

    def departure(u, v):
        return pltpu.make_async_copy(
            made_ref.at[:, u, v], out_ref.at[:, u, v], out_sem.at[u, v]
        )

    places = [(row, c) for row in range(rows) for c in range(2)]
    live_copy = pltpu.make_async_copy(live_ref, live_here, live_sem)
    live_copy.start()
    for place in places:
        arrival(*place).start()
    live_copy.wait()
    for place in places:
        arrival(*place).wait()
    right = right_ref[...].reshape(cols * rows * narrow, 2 * sides)
    for u in range(deep):
        for v in range(wide):
            live = live_here[u : u + 1, v : v + 1].astype(jnp.float32)
            real, imag = complex_dot(disaggregate_ref[0, u, v], disaggregate_ref[1, u, v], right)
            made_ref[0, u, v] = (near_ref[0, u, v] + real) * live
            made_ref[1, u, v] = (near_ref[1, u, v] + imag) * live
            departure(u, v).start()
    for u in range(deep):
        for v in range(wide):
            departure(u, v).wait()


def shards(unknowns, leaf_live, near_blocks, aggregate, disaggregate, translate):
    sect_count, dir_count = lax.axis_size("sect"), lax.axis_size("dir")
    _, deep, wide, size, sides = unknowns.shape
    total_dirs = aggregate.shape[3]
    narrow = total_dirs // (sect_count * dir_count)
    held = translate.shape[2]
    bf16, f32 = jnp.bfloat16, jnp.float32
    tiled = narrow % 16 == 0
    steps = 1
    rows, cols = (sect_count, dir_count) if tiled else (1, steps)
    block = total_dirs // (rows * cols)

    column = jax.ShapeDtypeStruct((2, deep, size, sides), bf16)
    corner = jax.ShapeDtypeStruct((2, size, sides), bf16)
    blocks = jax.ShapeDtypeStruct((rows, cols, 2, block, sides), bf16)
    whole = [
        pl.BlockSpec(a.shape, lambda i, n=len(a.shape): (0,) * n) for a in (unknowns, column, corner)
    ]
    patterns, col_near, col_cross, corner_near, corner_cross = pl.pallas_call(
        pattern_kernel,
        grid=(steps,),
        in_specs=[
            pl.BlockSpec(memory_space=pltpu.SMEM),
            whole[0],
            pl.BlockSpec((2, deep, wide, total_dirs // steps, size), lambda i: (0, 0, 0, i, 0)),
        ],
        out_specs=[
            pl.BlockSpec((rows, cols // steps, 2, block, sides), lambda i: (0, i, 0, 0, 0)),
            whole[1],
            whole[1],
            whole[2],
            whole[2],
        ],
        out_shape=[blocks, column, column, corner, corner],
        scratch_shapes=[pltpu.VMEM((deep * wide * size, 2 * sides), bf16)],
        compiler_params=params(),
        name="patterns",
    )(leaf_live, unknowns, aggregate)
    from_cross = swap_cols(col_cross, 1)
    from_near = swap_cols(col_near, 0)
    corner_near = swap_rows(corner_near, 0, 1)
    corner_cross = swap_rows(corner_cross, 1, 1)

    row = jax.ShapeDtypeStruct((2, 3, size, sides), bf16)
    row_near, row_cross = pl.pallas_call(
        row_kernel,
        in_specs=[ANY] * 3,
        out_specs=[ANY] * 2,
        out_shape=[row, row],
        scratch_shapes=[
            pltpu.VMEM((2, 3, 2, size, sides), bf16),
            pltpu.SemaphoreType.DMA((2, 6)),
        ],
        compiler_params=params(),
        cost_estimate=cost(8),
        name="rows",
    )(col_near, col_cross, from_cross)

    def spread(array):
        flat = array.reshape(rows * cols, 2, block, sides)
        return lax.all_to_all(flat, ("sect", "dir"), split_axis=0, concat_axis=0, tiled=True).reshape(array.shape)

    if tiled:
        own = spread(patterns)
        own, _, _ = lax.optimization_barrier((own, row_near, row_cross))
        lanes = min(128, sides)
        incoming = pl.pallas_call(
            translate_kernel,
            in_specs=[VMEM] * 2,
            out_specs=VMEM,
            out_shape=jax.ShapeDtypeStruct(own.shape, bf16),
            scratch_shapes=[
                pltpu.VMEM((held, 2 * len(far_offsets)), f32),
                pltpu.VMEM((2 * len(far_offsets), narrow, lanes), f32),
            ],
            compiler_params=params(16),
            cost_estimate=cost(8),
            name="translations",
        )(own, translate.reshape(2 * len(far_offsets), held))
        returned = spread(incoming)
    else:
        split = (2, dir_count, sect_count, narrow, sides)
        base = patterns[0].transpose(1, 0, 2, 3).reshape(split).transpose(0, 2, 1, 3, 4)
        base = base.reshape(2, total_dirs, sides)[None, None]
        own = lax.all_to_all(base, "sect", split_axis=3, concat_axis=0, tiled=True)
        own = lax.all_to_all(own, "dir", split_axis=3, concat_axis=1, tiled=True)
        coefs = lax.dynamic_slice_in_dim(translate, lax.axis_index("sect") * narrow, narrow, 2)
        incoming = translate_grid(own, coefs)
        returned = lax.all_to_all(incoming, "sect", split_axis=0, concat_axis=3, tiled=True)
        returned = lax.all_to_all(returned, "dir", split_axis=1, concat_axis=3, tiled=True)[0, 0]
        returned = returned.reshape(2, cols, block, sides).transpose(1, 0, 2, 3)[None]

    row_near = swap_rows(row_near, 0)
    row_cross = swap_rows(row_cross, 1)
    field = jax.ShapeDtypeStruct(unknowns.shape, f32)
    near = pl.pallas_call(
        near_kernel,
        grid=(deep * wide,),
        in_specs=[VMEM] * 8
        + [pl.BlockSpec((2, 1, 1, 9, size, size), lambda i: (0, i // wide, i % wide, 0, 0, 0))],
        out_specs=pl.BlockSpec((2, 1, 1, size, sides), lambda i: (0, i // wide, i % wide, 0, 0)),
        out_shape=field,
        scratch_shapes=[pltpu.VMEM((deep + 2, wide + 2, size, 2 * sides), bf16)],
        compiler_params=params(16),
        cost_estimate=cost(12),
        name="near",
    )(
        col_near, col_cross, from_cross, from_near, row_near, row_cross, corner_near, corner_cross,
        near_blocks,
    )
    return pl.pallas_call(
        far_kernel,
        in_specs=[ANY, ANY, VMEM, VMEM],
        out_specs=ANY,
        out_shape=field,
        scratch_shapes=[
            pltpu.VMEM(leaf_live.shape, jnp.int32),
            pltpu.VMEM((cols, rows, block, 2 * sides), bf16),
            pltpu.VMEM(unknowns.shape, f32),
            pltpu.SemaphoreType.DMA,
            pltpu.SemaphoreType.DMA((rows, 2)),
            pltpu.SemaphoreType.DMA((deep, wide)),
        ],
        compiler_params=params(16),
        name="far",
    )(leaf_live, returned, disaggregate, near)


def solution(mesh):
    in_specs = (
        P(None, "sect", "dir", None, None),
        P("sect", "dir"),
        P(None, "sect", "dir", None, None, None),
        P(None, "sect", "dir", None, None),
        P(None, "sect", "dir", None, None),
        P(None, None, "dir"),
    )
    out_specs = P(None, "sect", "dir", None, None)
    return jax.shard_map(shards, mesh=mesh, in_specs=in_specs, out_specs=out_specs, check_vma=False)
```

```python
import jax
import jax.numpy as jnp
from jax import lax
from jax.experimental import pallas as pl
from jax.experimental.pallas import tpu as pltpu
from jax.sharding import PartitionSpec as P

REACH = 2
MIB = 1 << 20
far_offsets = [
    (row_step, col_step)
    for row_step in range(-REACH, REACH + 1)
    for col_step in range(-REACH, REACH + 1)
    if max(abs(row_step), abs(col_step)) == REACH
]
VMEM = pl.BlockSpec(memory_space=pltpu.VMEM)
ANY = pl.BlockSpec(memory_space=pl.ANY)


def params(mib=56):
    return pltpu.CompilerParams(vmem_limit_bytes=mib * MIB)


def cost(micros):
    return pl.CostEstimate(flops=int(micros * 1.15e9), bytes_accessed=int(micros * 3.69e6), transcendentals=0)


def swap_pairs(count, first):
    pairs = []
    for i in range(count):
        partner = i + 1 if (i - first) % 2 == 0 else i - 1
        pairs.append((i, partner if 0 <= partner < count else None))
    return pairs


def swap_cols(array, first):
    rows, cols = lax.axis_size("sect"), lax.axis_size("dir")
    sends = []
    for row in range(rows):
        for col, partner in swap_pairs(cols, first):
            to = (row ^ 1) * cols + col if partner is None else row * cols + partner
            sends.append((row * cols + col, to))
    return lax.ppermute(array, ("sect", "dir"), sends)


def swap_rows(array, first, turn=0):
    rows, cols = lax.axis_size("sect"), lax.axis_size("dir")
    sends = []
    for row, partner in swap_pairs(rows, first):
        for col in range(cols):
            to = row * cols + (col ^ 1) if partner is None else partner * cols + (col ^ turn)
            sends.append((row * cols + col, to))
    return lax.ppermute(array, ("sect", "dir"), sends)


def complex_dot(left_real, left_imag, right):
    rows = left_real.shape[0]
    cols = right.shape[1] // 2
    both = jnp.dot(
        jnp.concatenate([left_real, left_imag], axis=0), right, preferred_element_type=jnp.float32
    )
    real = both[:rows, :cols] - both[rows:, cols:]
    imag = both[:rows, cols:] + both[rows:, :cols]
    return real, imag


def pattern_kernel(
    live_ref, unknowns_ref, aggregate_ref, out_ref, near_ref, cross_ref, corner_near_ref,
    corner_cross_ref, leaves_ref,
):
    rows, cols, _, narrow, sides = out_ref.shape
    deep, wide, size = unknowns_ref.shape[1:4]

    @pl.when(pl.program_id(0) == 0)
    def _():
        for u in range(deep):
            for v in range(wide):
                keep = live_ref[u, v].astype(jnp.float32).astype(jnp.bfloat16)
                at = (u * wide + v) * size
                for c in range(2):
                    leaves_ref[at : at + size, c * sides : (c + 1) * sides] = (
                        unknowns_ref[c, u, v] * keep
                    )

    left = [
        jnp.concatenate([aggregate_ref[c, u, v] for u in range(deep) for v in range(wide)], axis=1)
        for c in range(2)
    ]
    real, imag = complex_dot(left[0], left[1], leaves_ref[...])
    for row in range(rows):
        for col in range(cols):
            at = (col * rows + row) * narrow
            out_ref[row, col, 0] = real[at : at + narrow].astype(jnp.bfloat16)
            out_ref[row, col, 1] = imag[at : at + narrow].astype(jnp.bfloat16)

    @pl.when(pl.program_id(0) == 0)
    def _():
        odd = lax.rem(lax.axis_index("dir"), 2)
        row_odd = lax.rem(lax.axis_index("sect"), 2)

        def leaf(u, v, c):
            at = pl.multiple_of((u * wide + v) * size, size)
            return leaves_ref[pl.ds(at, size), c * sides : (c + 1) * sides]

        for c in range(2):
            for u in range(deep):
                near_ref[c, u] = leaf(u, 1 - odd, c)
                cross_ref[c, u] = leaf(u, odd, c)
            corner_near_ref[c] = leaf(1 - row_odd, 1 - odd, c)
            corner_cross_ref[c] = leaf(row_odd, 1 - odd, c)


def translate_kernel(from_ref, coef_ref, out_ref, turned_ref, wide_ref, held_ref):
    box_rows, box_cols, _, narrow, sides = from_ref.shape
    lanes = min(128, sides)

    turned_ref[...] = coef_ref[...].T
    first = pl.multiple_of(lax.axis_index("sect") * narrow, narrow)
    coefs = turned_ref[pl.ds(first, narrow)]
    for index in range(len(far_offsets)):
        real, imag = [
            jnp.broadcast_to(coefs[:, 2 * index + c : 2 * index + c + 1], (narrow, lanes)) for c in range(2)
        ]
        wide_ref[index, 0] = real
        wide_ref[index, 1] = imag
        wide_ref[index, 2] = real + imag

    def tile(place, carry):
        across = pl.ds(pl.multiple_of(place * lanes, lanes), lanes)
        real = from_ref[:, :, 0, :, across].astype(jnp.float32)
        imag = from_ref[:, :, 1, :, across].astype(jnp.float32)
        held_ref[:, :, 0] = real
        held_ref[:, :, 1] = imag
        held_ref[:, :, 2] = real + imag
        for col in range(box_cols):
            totals = [None] * box_rows
            for source in range(box_rows):
                held = {
                    step: [held_ref[source, col + step, k] for k in range(3)]
                    for step in range(-REACH, REACH + 1)
                    if 0 <= col + step < box_cols
                }
                for index, (row_step, step) in enumerate(far_offsets):
                    target = source - row_step
                    if 0 <= target < box_rows and step in held:
                        terms = [wide_ref[index, k] * held[step][k] for k in range(3)]
                        old = totals[target]
                        totals[target] = terms if old is None else [a + b for a, b in zip(old, terms)]
            for target, total in enumerate(totals):
                if total is None:
                    out_ref[target, col, :, :, across] = jnp.zeros((2, narrow, lanes), jnp.bfloat16)
                else:
                    a, b, c = total
                    out_ref[target, col, 0, :, across] = (a - b).astype(jnp.bfloat16)
                    out_ref[target, col, 1, :, across] = (c - a - b).astype(jnp.bfloat16)
        return carry

    lax.fori_loop(0, sides // lanes, tile, 0, unroll=True)


def translate_grid(sources, coefs):
    box_rows, box_cols = sources.shape[:2]
    widened = jnp.pad(sources.astype(jnp.float32), ((REACH, REACH), (REACH, REACH), (0, 0), (0, 0), (0, 0)))
    accum = jnp.zeros(sources.shape, jnp.float32)
    for row_step in range(-REACH, REACH + 1):
        total = jnp.zeros(sources.shape, jnp.float32)
        for index, (step_row, step_col) in enumerate(far_offsets):
            if step_row == row_step:
                shifted = widened[
                    REACH + step_row : REACH + step_row + box_rows,
                    REACH + step_col : REACH + step_col + box_cols,
                ]
                coef_real = coefs[index, 0][None, None, :, None]
                coef_imag = coefs[index, 1][None, None, :, None]
                real = coef_real * shifted[:, :, 0] - coef_imag * shifted[:, :, 1]
                imag = coef_real * shifted[:, :, 1] + coef_imag * shifted[:, :, 0]
                total = total + jnp.stack([real, imag], axis=2)
        accum = accum + total.astype(jnp.bfloat16).astype(jnp.float32)
    return accum.astype(jnp.bfloat16)


def move(copies, sem):
    arrivals = [
        pltpu.make_async_copy(source, held, sem.at[0, i]) for i, (source, held, _) in enumerate(copies)
    ]
    departures = [
        pltpu.make_async_copy(held, target, sem.at[1, i]) for i, (_, held, target) in enumerate(copies)
    ]
    for copy in arrivals:
        copy.start()
    for arrival, departure in zip(arrivals, departures):
        arrival.wait()
        departure.start()
    for copy in departures:
        copy.wait()


def row_kernel(near_ref, cross_ref, from_cross_ref, out_near_ref, out_cross_ref, held_ref, sem):
    odd = lax.rem(lax.axis_index("sect"), 2)
    copies = []
    for slot, ref in enumerate((near_ref, cross_ref, from_cross_ref)):
        copies.append((ref.at[:, 1 - odd], held_ref.at[0, slot], out_near_ref.at[:, slot]))
        copies.append((ref.at[:, odd], held_ref.at[1, slot], out_cross_ref.at[:, slot]))
    move(copies, sem)


def near_kernel(
    near_ref, cross_ref, from_cross_ref, from_near_ref, row_near_ref, row_cross_ref, corner_near_ref,
    corner_cross_ref, blocks_ref, out_ref, grid_ref,
):
    sides = near_ref.shape[3]
    deep = near_ref.shape[1]
    wide = 2
    leaf = pl.program_id(0)

    @pl.when(leaf == 0)
    def _():
        col_at, col_count = lax.axis_index("dir"), lax.axis_size("dir")
        row_at, row_count = lax.axis_index("sect"), lax.axis_size("sect")
        col_odd, row_odd = lax.rem(col_at, 2), lax.rem(row_at, 2)
        columns = (2 - col_odd, 1 + col_odd, 3 * col_odd, 3 - 3 * col_odd)
        row_next, row_last = 3 - 3 * row_odd, 3 * row_odd
        no_col = ((col_odd == 0) & (col_at == 0)) | ((col_odd == 1) & (col_at == col_count - 1))
        no_row = ((row_odd == 0) & (row_at == 0)) | ((row_odd == 1) & (row_at == row_count - 1))
        for slot, ref in enumerate((near_ref, cross_ref, from_cross_ref, from_near_ref)):
            for c in range(2):
                half = slice(c * sides, (c + 1) * sides)
                for u in range(deep):
                    grid_ref[1 + u, columns[slot], :, half] = ref[c, u]
                if slot < 3:
                    grid_ref[row_next, columns[slot], :, half] = row_near_ref[c, slot]
                    grid_ref[row_last, columns[slot], :, half] = row_cross_ref[c, slot]
                else:
                    grid_ref[row_next, columns[slot], :, half] = corner_near_ref[c]
                    grid_ref[row_last, columns[slot], :, half] = corner_cross_ref[c]

        @pl.when(no_col)
        def _():
            for i in range(deep + 2):
                grid_ref[i, columns[2]] = jnp.zeros(grid_ref.shape[2:], grid_ref.dtype)

        @pl.when(no_row)
        def _():
            for j in range(wide + 2):
                grid_ref[row_last, j] = jnp.zeros(grid_ref.shape[2:], grid_ref.dtype)

    u, v = leaf // wide, lax.rem(leaf, wide)
    right = jnp.concatenate(
        [grid_ref[u + a, v + b] for a in range(3) for b in range(3)], axis=0
    )
    left = [jnp.concatenate([blocks_ref[c, 0, 0, k] for k in range(9)], axis=1) for c in range(2)]
    real, imag = complex_dot(left[0], left[1], right)
    out_ref[0, 0, 0] = real
    out_ref[1, 0, 0] = imag


def far_kernel(
    live_ref, incoming_ref, disaggregate_ref, near_ref, out_ref, live_here, right_ref, made_ref, live_sem,
    in_sem, out_sem,
):
    rows, cols, _, narrow, sides = incoming_ref.shape
    deep, wide = live_ref.shape

    def arrival(row, c):
        return pltpu.make_async_copy(
            incoming_ref.at[row, :, c],
            right_ref.at[:, row, :, c * sides : (c + 1) * sides],
            in_sem.at[row, c],
        )

    def departure(u, v):
        return pltpu.make_async_copy(
            made_ref.at[:, u, v], out_ref.at[:, u, v], out_sem.at[u, v]
        )

    places = [(row, c) for row in range(rows) for c in range(2)]
    live_copy = pltpu.make_async_copy(live_ref, live_here, live_sem)
    live_copy.start()
    for place in places:
        arrival(*place).start()
    live_copy.wait()
    for place in places:
        arrival(*place).wait()
    right = right_ref[...].reshape(cols * rows * narrow, 2 * sides)
    for u in range(deep):
        for v in range(wide):
            live = live_here[u : u + 1, v : v + 1].astype(jnp.float32)
            real, imag = complex_dot(disaggregate_ref[0, u, v], disaggregate_ref[1, u, v], right)
            made_ref[0, u, v] = (near_ref[0, u, v] + real) * live
            made_ref[1, u, v] = (near_ref[1, u, v] + imag) * live
            departure(u, v).start()
    for u in range(deep):
        for v in range(wide):
            departure(u, v).wait()


def shards(unknowns, leaf_live, near_blocks, aggregate, disaggregate, translate):
    sect_count, dir_count = lax.axis_size("sect"), lax.axis_size("dir")
    _, deep, wide, size, sides = unknowns.shape
    total_dirs = aggregate.shape[3]
    narrow = total_dirs // (sect_count * dir_count)
    held = translate.shape[2]
    bf16, f32 = jnp.bfloat16, jnp.float32
    tiled = narrow % 16 == 0
    steps = 1
    rows, cols = (sect_count, dir_count) if tiled else (1, steps)
    block = total_dirs // (rows * cols)

    column = jax.ShapeDtypeStruct((2, deep, size, sides), bf16)
    corner = jax.ShapeDtypeStruct((2, size, sides), bf16)
    blocks = jax.ShapeDtypeStruct((rows, cols, 2, block, sides), bf16)
    whole = [
        pl.BlockSpec(a.shape, lambda i, n=len(a.shape): (0,) * n) for a in (unknowns, column, corner)
    ]
    patterns, col_near, col_cross, corner_near, corner_cross = pl.pallas_call(
        pattern_kernel,
        grid=(steps,),
        in_specs=[
            pl.BlockSpec(memory_space=pltpu.SMEM),
            whole[0],
            pl.BlockSpec((2, deep, wide, total_dirs // steps, size), lambda i: (0, 0, 0, i, 0)),
        ],
        out_specs=[
            pl.BlockSpec((rows, cols // steps, 2, block, sides), lambda i: (0, i, 0, 0, 0)),
            whole[1],
            whole[1],
            whole[2],
            whole[2],
        ],
        out_shape=[blocks, column, column, corner, corner],
        scratch_shapes=[pltpu.VMEM((deep * wide * size, 2 * sides), bf16)],
        compiler_params=params(),
        name="patterns",
    )(leaf_live, unknowns, aggregate)
    from_cross = swap_cols(col_cross, 1)
    from_near = swap_cols(col_near, 0)
    corner_near = swap_rows(corner_near, 0, 1)
    corner_cross = swap_rows(corner_cross, 1, 1)

    row = jax.ShapeDtypeStruct((2, 3, size, sides), bf16)
    row_near, row_cross = pl.pallas_call(
        row_kernel,
        in_specs=[ANY] * 3,
        out_specs=[ANY] * 2,
        out_shape=[row, row],
        scratch_shapes=[
            pltpu.VMEM((2, 3, 2, size, sides), bf16),
            pltpu.SemaphoreType.DMA((2, 6)),
        ],
        compiler_params=params(),
        cost_estimate=cost(8),
        name="rows",
    )(col_near, col_cross, from_cross)

    def spread(array):
        flat = array.reshape(rows * cols, 2, block, sides)
        return lax.all_to_all(flat, ("sect", "dir"), split_axis=0, concat_axis=0, tiled=True).reshape(array.shape)

    if tiled:
        own = spread(patterns)
        own, _, _ = lax.optimization_barrier((own, row_near, row_cross))
        lanes = min(128, sides)
        incoming = pl.pallas_call(
            translate_kernel,
            in_specs=[VMEM] * 2,
            out_specs=VMEM,
            out_shape=jax.ShapeDtypeStruct(own.shape, bf16),
            scratch_shapes=[
                pltpu.VMEM((held, 2 * len(far_offsets)), f32),
                pltpu.VMEM((len(far_offsets), 3, narrow, lanes), f32),
                pltpu.VMEM((rows, cols, 3, narrow, lanes), f32),
            ],
            compiler_params=params(16),
            cost_estimate=cost(8),
            name="translations",
        )(own, translate.reshape(2 * len(far_offsets), held))
        returned = spread(incoming)
    else:
        split = (2, dir_count, sect_count, narrow, sides)
        base = patterns[0].transpose(1, 0, 2, 3).reshape(split).transpose(0, 2, 1, 3, 4)
        base = base.reshape(2, total_dirs, sides)[None, None]
        own = lax.all_to_all(base, "sect", split_axis=3, concat_axis=0, tiled=True)
        own = lax.all_to_all(own, "dir", split_axis=3, concat_axis=1, tiled=True)
        coefs = lax.dynamic_slice_in_dim(translate, lax.axis_index("sect") * narrow, narrow, 2)
        incoming = translate_grid(own, coefs)
        returned = lax.all_to_all(incoming, "sect", split_axis=0, concat_axis=3, tiled=True)
        returned = lax.all_to_all(returned, "dir", split_axis=1, concat_axis=3, tiled=True)[0, 0]
        returned = returned.reshape(2, cols, block, sides).transpose(1, 0, 2, 3)[None]

    row_near = swap_rows(row_near, 0)
    row_cross = swap_rows(row_cross, 1)
    field = jax.ShapeDtypeStruct(unknowns.shape, f32)
    near = pl.pallas_call(
        near_kernel,
        grid=(deep * wide,),
        in_specs=[VMEM] * 8
        + [pl.BlockSpec((2, 1, 1, 9, size, size), lambda i: (0, i // wide, i % wide, 0, 0, 0))],
        out_specs=pl.BlockSpec((2, 1, 1, size, sides), lambda i: (0, i // wide, i % wide, 0, 0)),
        out_shape=field,
        scratch_shapes=[pltpu.VMEM((deep + 2, wide + 2, size, 2 * sides), bf16)],
        compiler_params=params(16),
        cost_estimate=cost(12),
        name="near",
    )(
        col_near, col_cross, from_cross, from_near, row_near, row_cross, corner_near, corner_cross,
        near_blocks,
    )
    return pl.pallas_call(
        far_kernel,
        in_specs=[ANY, ANY, VMEM, VMEM],
        out_specs=ANY,
        out_shape=field,
        scratch_shapes=[
            pltpu.VMEM(leaf_live.shape, jnp.int32),
            pltpu.VMEM((cols, rows, block, 2 * sides), bf16),
            pltpu.VMEM(unknowns.shape, f32),
            pltpu.SemaphoreType.DMA,
            pltpu.SemaphoreType.DMA((rows, 2)),
            pltpu.SemaphoreType.DMA((deep, wide)),
        ],
        compiler_params=params(16),
        name="far",
    )(leaf_live, returned, disaggregate, near)


def solution(mesh):
    in_specs = (
        P(None, "sect", "dir", None, None),
        P("sect", "dir"),
        P(None, "sect", "dir", None, None, None),
        P(None, "sect", "dir", None, None),
        P(None, "sect", "dir", None, None),
        P(None, None, "dir"),
    )
    out_specs = P(None, "sect", "dir", None, None)
    return jax.shard_map(shards, mesh=mesh, in_specs=in_specs, out_specs=out_specs, check_vma=False)
```

```python
import jax
import jax.numpy as jnp
from jax import lax
from jax.experimental import pallas as pl
from jax.experimental.pallas import tpu as pltpu
from jax.sharding import PartitionSpec as P

REACH = 2
MIB = 1 << 20
far_offsets = [
    (row_step, col_step)
    for row_step in range(-REACH, REACH + 1)
    for col_step in range(-REACH, REACH + 1)
    if max(abs(row_step), abs(col_step)) == REACH
]
VMEM = pl.BlockSpec(memory_space=pltpu.VMEM)
ANY = pl.BlockSpec(memory_space=pl.ANY)


def params(mib=56):
    return pltpu.CompilerParams(vmem_limit_bytes=mib * MIB)


def cost(micros):
    return pl.CostEstimate(flops=int(micros * 1.15e9), bytes_accessed=int(micros * 3.69e6), transcendentals=0)


def swap_pairs(count, first):
    pairs = []
    for i in range(count):
        partner = i + 1 if (i - first) % 2 == 0 else i - 1
        pairs.append((i, partner if 0 <= partner < count else None))
    return pairs


def swap_cols(array, first):
    rows, cols = lax.axis_size("sect"), lax.axis_size("dir")
    sends = []
    for row in range(rows):
        for col, partner in swap_pairs(cols, first):
            to = (row ^ 1) * cols + col if partner is None else row * cols + partner
            sends.append((row * cols + col, to))
    return lax.ppermute(array, ("sect", "dir"), sends)


def swap_rows(array, first, turn=0):
    rows, cols = lax.axis_size("sect"), lax.axis_size("dir")
    sends = []
    for row, partner in swap_pairs(rows, first):
        for col in range(cols):
            to = row * cols + (col ^ 1) if partner is None else partner * cols + (col ^ turn)
            sends.append((row * cols + col, to))
    return lax.ppermute(array, ("sect", "dir"), sends)


def complex_dot(left_real, left_imag, right):
    rows = left_real.shape[0]
    cols = right.shape[1] // 2
    both = jnp.dot(
        jnp.concatenate([left_real, left_imag], axis=0), right, preferred_element_type=jnp.float32
    )
    real = both[:rows, :cols] - both[rows:, cols:]
    imag = both[:rows, cols:] + both[rows:, :cols]
    return real, imag


def pattern_kernel(
    live_ref, unknowns_ref, aggregate_ref, out_ref, near_ref, cross_ref, corner_near_ref,
    corner_cross_ref, leaves_ref,
):
    parts, _, narrow, sides = out_ref.shape
    deep, wide, size = unknowns_ref.shape[1:4]

    for u in range(deep):
        for v in range(wide):
            keep = live_ref[u, v].astype(jnp.float32).astype(jnp.bfloat16)
            at = (u * wide + v) * size
            for c in range(2):
                leaves_ref[at : at + size, c * sides : (c + 1) * sides] = (
                    unknowns_ref[c, u, v] * keep
                )

    left = [
        jnp.concatenate([aggregate_ref[c, u, v] for u in range(deep) for v in range(wide)], axis=1)
        for c in range(2)
    ]
    real, imag = complex_dot(left[0], left[1], leaves_ref[...])
    for part in range(parts):
        out_ref[part, 0] = real[part * narrow : (part + 1) * narrow].astype(jnp.bfloat16)
        out_ref[part, 1] = imag[part * narrow : (part + 1) * narrow].astype(jnp.bfloat16)

    odd = lax.rem(lax.axis_index("dir"), 2)
    row_odd = lax.rem(lax.axis_index("sect"), 2)

    def leaf(u, v, c):
        at = pl.multiple_of((u * wide + v) * size, size)
        return leaves_ref[pl.ds(at, size), c * sides : (c + 1) * sides]

    for c in range(2):
        for u in range(deep):
            near_ref[c, u] = leaf(u, 1 - odd, c)
            cross_ref[c, u] = leaf(u, odd, c)
        corner_near_ref[c] = leaf(1 - row_odd, 1 - odd, c)
        corner_cross_ref[c] = leaf(row_odd, 1 - odd, c)


def translate_kernel(from_ref, coef_ref, out_ref, turned_ref, wide_ref, held_ref):
    box_cols, box_rows, _, narrow, sides = from_ref.shape
    lanes = min(128, sides)

    turned_ref[...] = coef_ref[...].T
    first = pl.multiple_of(lax.axis_index("sect") * narrow, narrow)
    coefs = turned_ref[pl.ds(first, narrow)]
    for index in range(len(far_offsets)):
        real, imag = [
            jnp.broadcast_to(coefs[:, 2 * index + c : 2 * index + c + 1], (narrow, lanes)) for c in range(2)
        ]
        wide_ref[index, 0] = real
        wide_ref[index, 1] = imag
        wide_ref[index, 2] = real + imag

    def tile(place, carry):
        across = pl.ds(pl.multiple_of(place * lanes, lanes), lanes)
        real = from_ref[:, :, 0, :, across].astype(jnp.float32)
        imag = from_ref[:, :, 1, :, across].astype(jnp.float32)
        held_ref[:, :, 0] = real
        held_ref[:, :, 1] = imag
        held_ref[:, :, 2] = real + imag
        for col in range(box_cols):
            totals = [None] * box_rows
            for source in range(box_rows):
                held = {
                    step: [held_ref[col + step, source, k] for k in range(3)]
                    for step in range(-REACH, REACH + 1)
                    if 0 <= col + step < box_cols
                }
                for target in range(max(0, source - REACH), min(box_rows, source + REACH + 1)):
                    sums = None
                    for index, (row_step, step) in enumerate(far_offsets):
                        if row_step == source - target and step in held:
                            terms = [wide_ref[index, k] * held[step][k] for k in range(3)]
                            sums = terms if sums is None else [x + y for x, y in zip(sums, terms)]
                    if sums is None:
                        continue
                    a, b, c = sums
                    term = [x.astype(jnp.bfloat16).astype(jnp.float32) for x in (a - b, c - a - b)]
                    old = totals[target]
                    totals[target] = term if old is None else [x + y for x, y in zip(old, term)]
            for target, total in enumerate(totals):
                for c in range(2):
                    out_ref[col, target, c, :, across] = (
                        jnp.zeros((narrow, lanes), jnp.bfloat16)
                        if total is None
                        else total[c].astype(jnp.bfloat16)
                    )
        return carry

    lax.fori_loop(0, sides // lanes, tile, 0, unroll=True)


def translate_grid(sources, coefs):
    box_rows, box_cols = sources.shape[:2]
    widened = jnp.pad(sources.astype(jnp.float32), ((REACH, REACH), (REACH, REACH), (0, 0), (0, 0), (0, 0)))
    accum = jnp.zeros(sources.shape, jnp.float32)
    for row_step in range(-REACH, REACH + 1):
        total = jnp.zeros(sources.shape, jnp.float32)
        for index, (step_row, step_col) in enumerate(far_offsets):
            if step_row == row_step:
                shifted = widened[
                    REACH + step_row : REACH + step_row + box_rows,
                    REACH + step_col : REACH + step_col + box_cols,
                ]
                coef_real = coefs[index, 0][None, None, :, None]
                coef_imag = coefs[index, 1][None, None, :, None]
                real = coef_real * shifted[:, :, 0] - coef_imag * shifted[:, :, 1]
                imag = coef_real * shifted[:, :, 1] + coef_imag * shifted[:, :, 0]
                total = total + jnp.stack([real, imag], axis=2)
        accum = accum + total.astype(jnp.bfloat16).astype(jnp.float32)
    return accum.astype(jnp.bfloat16)


def move(copies, sem):
    arrivals = [
        pltpu.make_async_copy(source, held, sem.at[0, i]) for i, (source, held, _) in enumerate(copies)
    ]
    departures = [
        pltpu.make_async_copy(held, target, sem.at[1, i]) for i, (_, held, target) in enumerate(copies)
    ]
    for copy in arrivals:
        copy.start()
    for arrival, departure in zip(arrivals, departures):
        arrival.wait()
        departure.start()
    for copy in departures:
        copy.wait()


def row_kernel(near_ref, cross_ref, from_cross_ref, out_near_ref, out_cross_ref, held_ref, sem):
    odd = lax.rem(lax.axis_index("sect"), 2)
    copies = []
    for slot, ref in enumerate((near_ref, cross_ref, from_cross_ref)):
        copies.append((ref.at[:, 1 - odd], held_ref.at[0, slot], out_near_ref.at[:, slot]))
        copies.append((ref.at[:, odd], held_ref.at[1, slot], out_cross_ref.at[:, slot]))
    move(copies, sem)


def near_kernel(
    near_ref, cross_ref, from_cross_ref, from_near_ref, row_near_ref, row_cross_ref, corner_near_ref,
    corner_cross_ref, blocks_ref, out_ref, grid_ref,
):
    sides = near_ref.shape[3]
    deep = near_ref.shape[1]
    wide = 2
    leaf = pl.program_id(0)

    @pl.when(leaf == 0)
    def _():
        col_at, col_count = lax.axis_index("dir"), lax.axis_size("dir")
        row_at, row_count = lax.axis_index("sect"), lax.axis_size("sect")
        col_odd, row_odd = lax.rem(col_at, 2), lax.rem(row_at, 2)
        columns = (2 - col_odd, 1 + col_odd, 3 * col_odd, 3 - 3 * col_odd)
        row_next, row_last = 3 - 3 * row_odd, 3 * row_odd
        no_col = ((col_odd == 0) & (col_at == 0)) | ((col_odd == 1) & (col_at == col_count - 1))
        no_row = ((row_odd == 0) & (row_at == 0)) | ((row_odd == 1) & (row_at == row_count - 1))
        for slot, ref in enumerate((near_ref, cross_ref, from_cross_ref, from_near_ref)):
            for c in range(2):
                half = slice(c * sides, (c + 1) * sides)
                for u in range(deep):
                    grid_ref[1 + u, columns[slot], :, half] = ref[c, u]
                if slot < 3:
                    grid_ref[row_next, columns[slot], :, half] = row_near_ref[c, slot]
                    grid_ref[row_last, columns[slot], :, half] = row_cross_ref[c, slot]
                else:
                    grid_ref[row_next, columns[slot], :, half] = corner_near_ref[c]
                    grid_ref[row_last, columns[slot], :, half] = corner_cross_ref[c]

        @pl.when(no_col)
        def _():
            for i in range(deep + 2):
                grid_ref[i, columns[2]] = jnp.zeros(grid_ref.shape[2:], grid_ref.dtype)

        @pl.when(no_row)
        def _():
            for j in range(wide + 2):
                grid_ref[row_last, j] = jnp.zeros(grid_ref.shape[2:], grid_ref.dtype)

    u, v = leaf // wide, lax.rem(leaf, wide)
    right = jnp.concatenate(
        [grid_ref[u + a, v + b] for a in range(3) for b in range(3)], axis=0
    )
    left = [jnp.concatenate([blocks_ref[c, 0, 0, k] for k in range(9)], axis=1) for c in range(2)]
    real, imag = complex_dot(left[0], left[1], right)
    out_ref[0, 0, 0] = real
    out_ref[1, 0, 0] = imag


def far_kernel(
    live_ref, incoming_ref, disaggregate_ref, near_ref, out_ref, live_here, right_ref, made_ref, live_sem,
    in_sem, out_sem,
):
    parts, _, narrow, sides = incoming_ref.shape
    deep, wide = live_ref.shape

    def arrival(c):
        return pltpu.make_async_copy(
            incoming_ref.at[:, c], right_ref.at[:, :, c * sides : (c + 1) * sides], in_sem.at[c]
        )

    def departure(u, v):
        return pltpu.make_async_copy(
            made_ref.at[:, u, v], out_ref.at[:, u, v], out_sem.at[u, v]
        )

    live_copy = pltpu.make_async_copy(live_ref, live_here, live_sem)
    live_copy.start()
    for c in range(2):
        arrival(c).start()
    live_copy.wait()
    for c in range(2):
        arrival(c).wait()
    right = right_ref[...].reshape(parts * narrow, 2 * sides)
    for u in range(deep):
        for v in range(wide):
            live = live_here[u : u + 1, v : v + 1].astype(jnp.float32)
            real, imag = complex_dot(disaggregate_ref[0, u, v], disaggregate_ref[1, u, v], right)
            made_ref[0, u, v] = (near_ref[0, u, v] + real) * live
            made_ref[1, u, v] = (near_ref[1, u, v] + imag) * live
            departure(u, v).start()
    for u in range(deep):
        for v in range(wide):
            departure(u, v).wait()


def shards(unknowns, leaf_live, near_blocks, aggregate, disaggregate, translate):
    sect_count, dir_count = lax.axis_size("sect"), lax.axis_size("dir")
    _, deep, wide, size, sides = unknowns.shape
    total_dirs = aggregate.shape[3]
    narrow = total_dirs // (sect_count * dir_count)
    held = translate.shape[2]
    bf16, f32 = jnp.bfloat16, jnp.float32
    tiled = narrow % 16 == 0
    parts = dir_count * sect_count if tiled else 1
    block = total_dirs // parts

    column = jax.ShapeDtypeStruct((2, deep, size, sides), bf16)
    corner = jax.ShapeDtypeStruct((2, size, sides), bf16)
    blocks = jax.ShapeDtypeStruct((parts, 2, block, sides), bf16)
    patterns, col_near, col_cross, corner_near, corner_cross = pl.pallas_call(
        pattern_kernel,
        in_specs=[pl.BlockSpec(memory_space=pltpu.SMEM), VMEM, VMEM],
        out_specs=[VMEM] * 5,
        out_shape=[blocks, column, column, corner, corner],
        scratch_shapes=[pltpu.VMEM((deep * wide * size, 2 * sides), bf16)],
        compiler_params=params(),
        name="patterns",
    )(leaf_live, unknowns, aggregate)
    from_cross = swap_cols(col_cross, 1)
    from_near = swap_cols(col_near, 0)
    corner_near = swap_rows(corner_near, 0, 1)
    corner_cross = swap_rows(corner_cross, 1, 1)

    row = jax.ShapeDtypeStruct((2, 3, size, sides), bf16)
    row_near, row_cross = pl.pallas_call(
        row_kernel,
        in_specs=[ANY] * 3,
        out_specs=[ANY] * 2,
        out_shape=[row, row],
        scratch_shapes=[
            pltpu.VMEM((2, 3, 2, size, sides), bf16),
            pltpu.SemaphoreType.DMA((2, 6)),
        ],
        compiler_params=params(),
        cost_estimate=cost(8),
        name="rows",
    )(col_near, col_cross, from_cross)

    def spread(array):
        flat = array.reshape(parts, 2, block, sides)
        return lax.all_to_all(flat, ("dir", "sect"), split_axis=0, concat_axis=0, tiled=True)

    if tiled:
        own = spread(patterns).reshape(dir_count, sect_count, 2, block, sides)
        own, _, _ = lax.optimization_barrier((own, row_near, row_cross))
        lanes = min(128, sides)
        incoming = pl.pallas_call(
            translate_kernel,
            in_specs=[VMEM] * 2,
            out_specs=VMEM,
            out_shape=jax.ShapeDtypeStruct(own.shape, bf16),
            scratch_shapes=[
                pltpu.VMEM((held, 2 * len(far_offsets)), f32),
                pltpu.VMEM((len(far_offsets), 3, narrow, lanes), f32),
                pltpu.VMEM((dir_count, sect_count, 3, narrow, lanes), f32),
            ],
            compiler_params=params(16),
            cost_estimate=cost(8),
            name="translations",
        )(own, translate.reshape(2 * len(far_offsets), held))
        returned = spread(incoming)
    else:
        base = patterns.reshape(2, dir_count, sect_count, narrow, sides).transpose(0, 2, 1, 3, 4)
        base = base.reshape(2, total_dirs, sides)[None, None]
        own = lax.all_to_all(base, "sect", split_axis=3, concat_axis=0, tiled=True)
        own = lax.all_to_all(own, "dir", split_axis=3, concat_axis=1, tiled=True)
        coefs = lax.dynamic_slice_in_dim(translate, lax.axis_index("sect") * narrow, narrow, 2)
        incoming = translate_grid(own, coefs)
        returned = lax.all_to_all(incoming, "sect", split_axis=0, concat_axis=3, tiled=True)
        returned = lax.all_to_all(returned, "dir", split_axis=1, concat_axis=3, tiled=True)[0]

    row_near = swap_rows(row_near, 0)
    row_cross = swap_rows(row_cross, 1)
    field = jax.ShapeDtypeStruct(unknowns.shape, f32)
    near = pl.pallas_call(
        near_kernel,
        grid=(deep * wide,),
        in_specs=[VMEM] * 8
        + [pl.BlockSpec((2, 1, 1, 9, size, size), lambda i: (0, i // wide, i % wide, 0, 0, 0))],
        out_specs=pl.BlockSpec((2, 1, 1, size, sides), lambda i: (0, i // wide, i % wide, 0, 0)),
        out_shape=field,
        scratch_shapes=[pltpu.VMEM((deep + 2, wide + 2, size, 2 * sides), bf16)],
        compiler_params=params(16),
        cost_estimate=cost(12),
        name="near",
    )(
        col_near, col_cross, from_cross, from_near, row_near, row_cross, corner_near, corner_cross,
        near_blocks,
    )
    return pl.pallas_call(
        far_kernel,
        in_specs=[ANY, ANY, VMEM, VMEM],
        out_specs=ANY,
        out_shape=field,
        scratch_shapes=[
            pltpu.VMEM(leaf_live.shape, jnp.int32),
            pltpu.VMEM((parts, block, 2 * sides), bf16),
            pltpu.VMEM(unknowns.shape, f32),
            pltpu.SemaphoreType.DMA,
            pltpu.SemaphoreType.DMA((2,)),
            pltpu.SemaphoreType.DMA((deep, wide)),
        ],
        compiler_params=params(16),
        name="far",
    )(leaf_live, returned, disaggregate, near)


def solution(mesh):
    in_specs = (
        P(None, "sect", "dir", None, None),
        P("sect", "dir"),
        P(None, "sect", "dir", None, None, None),
        P(None, "sect", "dir", None, None),
        P(None, "sect", "dir", None, None),
        P(None, None, "dir"),
    )
    out_specs = P(None, "sect", "dir", None, None)
    return jax.shard_map(shards, mesh=mesh, in_specs=in_specs, out_specs=out_specs, check_vma=False)
```

```python
import jax
import jax.numpy as jnp
from jax import lax
from jax.experimental import pallas as pl
from jax.experimental.pallas import tpu as pltpu
from jax.sharding import PartitionSpec as P

REACH = 2
MIB = 1 << 20
far_offsets = [
    (row_step, col_step)
    for row_step in range(-REACH, REACH + 1)
    for col_step in range(-REACH, REACH + 1)
    if max(abs(row_step), abs(col_step)) == REACH
]
VMEM = pl.BlockSpec(memory_space=pltpu.VMEM)
ANY = pl.BlockSpec(memory_space=pl.ANY)


def params(mib=56):
    return pltpu.CompilerParams(vmem_limit_bytes=mib * MIB)


def cost(micros):
    return pl.CostEstimate(flops=int(micros * 1.15e9), bytes_accessed=int(micros * 3.69e6), transcendentals=0)


def swap_pairs(count, first):
    pairs = []
    for i in range(count):
        partner = i + 1 if (i - first) % 2 == 0 else i - 1
        pairs.append((i, partner if 0 <= partner < count else None))
    return pairs


def swap_cols(array, first):
    rows, cols = lax.axis_size("sect"), lax.axis_size("dir")
    sends = []
    for row in range(rows):
        for col, partner in swap_pairs(cols, first):
            to = (row ^ 1) * cols + col if partner is None else row * cols + partner
            sends.append((row * cols + col, to))
    return lax.ppermute(array, ("sect", "dir"), sends)


def swap_rows(array, first, turn=0):
    rows, cols = lax.axis_size("sect"), lax.axis_size("dir")
    sends = []
    for row, partner in swap_pairs(rows, first):
        for col in range(cols):
            to = row * cols + (col ^ 1) if partner is None else partner * cols + (col ^ turn)
            sends.append((row * cols + col, to))
    return lax.ppermute(array, ("sect", "dir"), sends)


def complex_dot(left_real, left_imag, right):
    rows = left_real.shape[0]
    cols = right.shape[1] // 2
    both = jnp.dot(
        jnp.concatenate([left_real, left_imag], axis=0), right, preferred_element_type=jnp.float32
    )
    real = both[:rows, :cols] - both[rows:, cols:]
    imag = both[:rows, cols:] + both[rows:, :cols]
    return real, imag


def pattern_kernel(
    live_ref, unknowns_ref, aggregate_ref, out_ref, near_ref, cross_ref, corner_near_ref,
    corner_cross_ref, leaves_ref,
):
    parts, _, narrow, sides = out_ref.shape
    deep, wide, size = unknowns_ref.shape[1:4]

    for u in range(deep):
        for v in range(wide):
            keep = live_ref[u, v].astype(jnp.float32).astype(jnp.bfloat16)
            at = (u * wide + v) * size
            for c in range(2):
                leaves_ref[at : at + size, c * sides : (c + 1) * sides] = (
                    unknowns_ref[c, u, v] * keep
                )

    left = [
        jnp.concatenate([aggregate_ref[c, u, v] for u in range(deep) for v in range(wide)], axis=1)
        for c in range(2)
    ]
    real, imag = complex_dot(left[0], left[1], leaves_ref[...])
    for part in range(parts):
        out_ref[part, 0] = real[part * narrow : (part + 1) * narrow].astype(jnp.bfloat16)
        out_ref[part, 1] = imag[part * narrow : (part + 1) * narrow].astype(jnp.bfloat16)

    odd = lax.rem(lax.axis_index("dir"), 2)
    row_odd = lax.rem(lax.axis_index("sect"), 2)

    def leaf(u, v, c):
        at = pl.multiple_of((u * wide + v) * size, size)
        return leaves_ref[pl.ds(at, size), c * sides : (c + 1) * sides]

    for c in range(2):
        for u in range(deep):
            near_ref[c, u] = leaf(u, 1 - odd, c)
            cross_ref[c, u] = leaf(u, odd, c)
        corner_near_ref[c] = leaf(1 - row_odd, 1 - odd, c)
        corner_cross_ref[c] = leaf(row_odd, 1 - odd, c)


def translate_kernel(from_ref, coef_ref, out_ref, turned_ref, wide_ref, held_ref):
    box_cols, box_rows, _, narrow, sides = from_ref.shape
    lanes = min(128, sides)

    turned_ref[...] = coef_ref[...].T
    first = pl.multiple_of(lax.axis_index("sect") * narrow, narrow)
    coefs = turned_ref[pl.ds(first, narrow)]
    for index in range(len(far_offsets)):
        real, imag = [
            jnp.broadcast_to(coefs[:, 2 * index + c : 2 * index + c + 1], (narrow, lanes)) for c in range(2)
        ]
        wide_ref[index, 0] = real
        wide_ref[index, 1] = imag
        wide_ref[index, 2] = real + imag

    def tile(place, carry):
        across = pl.ds(pl.multiple_of(place * lanes, lanes), lanes)
        real = from_ref[:, :, 0, :, across].astype(jnp.float32)
        imag = from_ref[:, :, 1, :, across].astype(jnp.float32)
        held_ref[:, :, 0] = real
        held_ref[:, :, 1] = imag
        held_ref[:, :, 2] = real + imag
        for col in range(box_cols):
            totals = [None] * box_rows
            for source in range(box_rows):
                held = {
                    step: [held_ref[col + step, source, k] for k in range(3)]
                    for step in range(-REACH, REACH + 1)
                    if 0 <= col + step < box_cols
                }
                for target in range(max(0, source - REACH), min(box_rows, source + REACH + 1)):
                    sums = None
                    for index, (row_step, step) in enumerate(far_offsets):
                        if row_step == source - target and step in held:
                            terms = [wide_ref[index, k] * held[step][k] for k in range(3)]
                            sums = terms if sums is None else [x + y for x, y in zip(sums, terms)]
                    if sums is None:
                        continue
                    a, b, c = sums
                    term = [x.astype(jnp.bfloat16).astype(jnp.float32) for x in (a - b, c - a - b)]
                    old = totals[target]
                    totals[target] = term if old is None else [x + y for x, y in zip(old, term)]
            for target, total in enumerate(totals):
                for c in range(2):
                    out_ref[col, target, c, :, across] = (
                        jnp.zeros((narrow, lanes), jnp.bfloat16)
                        if total is None
                        else total[c].astype(jnp.bfloat16)
                    )
        return carry

    lax.fori_loop(0, sides // lanes, tile, 0, unroll=True)


def translate_grid(sources, coefs):
    box_rows, box_cols = sources.shape[:2]
    widened = jnp.pad(sources.astype(jnp.float32), ((REACH, REACH), (REACH, REACH), (0, 0), (0, 0), (0, 0)))
    accum = jnp.zeros(sources.shape, jnp.float32)
    for row_step in range(-REACH, REACH + 1):
        total = jnp.zeros(sources.shape, jnp.float32)
        for index, (step_row, step_col) in enumerate(far_offsets):
            if step_row == row_step:
                shifted = widened[
                    REACH + step_row : REACH + step_row + box_rows,
                    REACH + step_col : REACH + step_col + box_cols,
                ]
                coef_real = coefs[index, 0][None, None, :, None]
                coef_imag = coefs[index, 1][None, None, :, None]
                real = coef_real * shifted[:, :, 0] - coef_imag * shifted[:, :, 1]
                imag = coef_real * shifted[:, :, 1] + coef_imag * shifted[:, :, 0]
                total = total + jnp.stack([real, imag], axis=2)
        accum = accum + total.astype(jnp.bfloat16).astype(jnp.float32)
    return accum.astype(jnp.bfloat16)


def move(copies, sem):
    arrivals = [
        pltpu.make_async_copy(source, held, sem.at[0, i]) for i, (source, held, _) in enumerate(copies)
    ]
    departures = [
        pltpu.make_async_copy(held, target, sem.at[1, i]) for i, (_, held, target) in enumerate(copies)
    ]
    for copy in arrivals:
        copy.start()
    for arrival, departure in zip(arrivals, departures):
        arrival.wait()
        departure.start()
    for copy in departures:
        copy.wait()


def row_kernel(near_ref, cross_ref, from_cross_ref, out_near_ref, out_cross_ref, held_ref, sem):
    odd = lax.rem(lax.axis_index("sect"), 2)
    copies = []
    for slot, ref in enumerate((near_ref, cross_ref, from_cross_ref)):
        copies.append((ref.at[:, 1 - odd], held_ref.at[0, slot], out_near_ref.at[:, slot]))
        copies.append((ref.at[:, odd], held_ref.at[1, slot], out_cross_ref.at[:, slot]))
    move(copies, sem)


def near_kernel(
    near_ref, cross_ref, from_cross_ref, from_near_ref, row_near_ref, row_cross_ref, corner_near_ref,
    corner_cross_ref, blocks_ref, out_ref, grid_ref,
):
    sides = near_ref.shape[3]
    deep = near_ref.shape[1]
    wide = 2
    leaf = pl.program_id(0)

    @pl.when(leaf == 0)
    def _():
        col_at, col_count = lax.axis_index("dir"), lax.axis_size("dir")
        row_at, row_count = lax.axis_index("sect"), lax.axis_size("sect")
        col_odd, row_odd = lax.rem(col_at, 2), lax.rem(row_at, 2)
        columns = (2 - col_odd, 1 + col_odd, 3 * col_odd, 3 - 3 * col_odd)
        row_next, row_last = 3 - 3 * row_odd, 3 * row_odd
        no_col = ((col_odd == 0) & (col_at == 0)) | ((col_odd == 1) & (col_at == col_count - 1))
        no_row = ((row_odd == 0) & (row_at == 0)) | ((row_odd == 1) & (row_at == row_count - 1))
        for slot, ref in enumerate((near_ref, cross_ref, from_cross_ref, from_near_ref)):
            for c in range(2):
                half = slice(c * sides, (c + 1) * sides)
                for u in range(deep):
                    grid_ref[1 + u, columns[slot], :, half] = ref[c, u]
                if slot < 3:
                    grid_ref[row_next, columns[slot], :, half] = row_near_ref[c, slot]
                    grid_ref[row_last, columns[slot], :, half] = row_cross_ref[c, slot]
                else:
                    grid_ref[row_next, columns[slot], :, half] = corner_near_ref[c]
                    grid_ref[row_last, columns[slot], :, half] = corner_cross_ref[c]

        @pl.when(no_col)
        def _():
            for i in range(deep + 2):
                grid_ref[i, columns[2]] = jnp.zeros(grid_ref.shape[2:], grid_ref.dtype)

        @pl.when(no_row)
        def _():
            for j in range(wide + 2):
                grid_ref[row_last, j] = jnp.zeros(grid_ref.shape[2:], grid_ref.dtype)

    u, v = leaf // wide, lax.rem(leaf, wide)
    right = jnp.concatenate(
        [grid_ref[u + a, v + b] for a in range(3) for b in range(3)], axis=0
    )
    left = [jnp.concatenate([blocks_ref[c, 0, 0, k] for k in range(9)], axis=1) for c in range(2)]
    real, imag = complex_dot(left[0], left[1], right)
    out_ref[0, 0, 0] = real
    out_ref[1, 0, 0] = imag


def far_kernel(
    live_ref, incoming_ref, disaggregate_ref, near_ref, out_ref, live_here, right_ref, made_ref, live_sem,
    out_sem,
):
    parts, _, narrow, sides = incoming_ref.shape
    deep, wide = live_ref.shape

    def departure(u, v):
        return pltpu.make_async_copy(
            made_ref.at[:, u, v], out_ref.at[:, u, v], out_sem.at[u, v]
        )

    live_copy = pltpu.make_async_copy(live_ref, live_here, live_sem)
    live_copy.start()
    for c in range(2):
        right_ref[:, :, c * sides : (c + 1) * sides] = incoming_ref[:, c]
    live_copy.wait()
    right = right_ref[...].reshape(parts * narrow, 2 * sides)
    for u in range(deep):
        for v in range(wide):
            live = live_here[u : u + 1, v : v + 1].astype(jnp.float32)
            real, imag = complex_dot(disaggregate_ref[0, u, v], disaggregate_ref[1, u, v], right)
            made_ref[0, u, v] = (near_ref[0, u, v] + real) * live
            made_ref[1, u, v] = (near_ref[1, u, v] + imag) * live
            departure(u, v).start()
    for u in range(deep):
        for v in range(wide):
            departure(u, v).wait()


def shards(unknowns, leaf_live, near_blocks, aggregate, disaggregate, translate):
    sect_count, dir_count = lax.axis_size("sect"), lax.axis_size("dir")
    _, deep, wide, size, sides = unknowns.shape
    total_dirs = aggregate.shape[3]
    narrow = total_dirs // (sect_count * dir_count)
    held = translate.shape[2]
    bf16, f32 = jnp.bfloat16, jnp.float32
    tiled = narrow % 16 == 0
    parts = dir_count * sect_count if tiled else 1
    block = total_dirs // parts

    column = jax.ShapeDtypeStruct((2, deep, size, sides), bf16)
    corner = jax.ShapeDtypeStruct((2, size, sides), bf16)
    blocks = jax.ShapeDtypeStruct((parts, 2, block, sides), bf16)
    patterns, col_near, col_cross, corner_near, corner_cross = pl.pallas_call(
        pattern_kernel,
        in_specs=[pl.BlockSpec(memory_space=pltpu.SMEM), VMEM, VMEM],
        out_specs=[VMEM] * 5,
        out_shape=[blocks, column, column, corner, corner],
        scratch_shapes=[pltpu.VMEM((deep * wide * size, 2 * sides), bf16)],
        compiler_params=params(),
        name="patterns",
    )(leaf_live, unknowns, aggregate)
    from_cross = swap_cols(col_cross, 1)
    from_near = swap_cols(col_near, 0)
    corner_near = swap_rows(corner_near, 0, 1)
    corner_cross = swap_rows(corner_cross, 1, 1)

    row = jax.ShapeDtypeStruct((2, 3, size, sides), bf16)
    row_near, row_cross = pl.pallas_call(
        row_kernel,
        in_specs=[ANY] * 3,
        out_specs=[ANY] * 2,
        out_shape=[row, row],
        scratch_shapes=[
            pltpu.VMEM((2, 3, 2, size, sides), bf16),
            pltpu.SemaphoreType.DMA((2, 6)),
        ],
        compiler_params=params(),
        cost_estimate=cost(8),
        name="rows",
    )(col_near, col_cross, from_cross)

    def spread(array):
        flat = array.reshape(parts, 2, block, sides)
        return lax.all_to_all(flat, ("dir", "sect"), split_axis=0, concat_axis=0, tiled=True)

    if tiled:
        own = spread(patterns).reshape(dir_count, sect_count, 2, block, sides)
        own, _, _ = lax.optimization_barrier((own, row_near, row_cross))
        lanes = min(128, sides)
        incoming = pl.pallas_call(
            translate_kernel,
            in_specs=[VMEM] * 2,
            out_specs=VMEM,
            out_shape=jax.ShapeDtypeStruct(own.shape, bf16),
            scratch_shapes=[
                pltpu.VMEM((held, 2 * len(far_offsets)), f32),
                pltpu.VMEM((len(far_offsets), 3, narrow, lanes), f32),
                pltpu.VMEM((dir_count, sect_count, 3, narrow, lanes), f32),
            ],
            compiler_params=params(16),
            cost_estimate=cost(8),
            name="translations",
        )(own, translate.reshape(2 * len(far_offsets), held))
        returned = spread(incoming)
    else:
        base = patterns.reshape(2, dir_count, sect_count, narrow, sides).transpose(0, 2, 1, 3, 4)
        base = base.reshape(2, total_dirs, sides)[None, None]
        own = lax.all_to_all(base, "sect", split_axis=3, concat_axis=0, tiled=True)
        own = lax.all_to_all(own, "dir", split_axis=3, concat_axis=1, tiled=True)
        coefs = lax.dynamic_slice_in_dim(translate, lax.axis_index("sect") * narrow, narrow, 2)
        incoming = translate_grid(own, coefs)
        returned = lax.all_to_all(incoming, "sect", split_axis=0, concat_axis=3, tiled=True)
        returned = lax.all_to_all(returned, "dir", split_axis=1, concat_axis=3, tiled=True)[0]

    row_near = swap_rows(row_near, 0)
    row_cross = swap_rows(row_cross, 1)
    field = jax.ShapeDtypeStruct(unknowns.shape, f32)
    near = pl.pallas_call(
        near_kernel,
        grid=(deep * wide,),
        in_specs=[VMEM] * 8
        + [pl.BlockSpec((2, 1, 1, 9, size, size), lambda i: (0, i // wide, i % wide, 0, 0, 0))],
        out_specs=pl.BlockSpec((2, 1, 1, size, sides), lambda i: (0, i // wide, i % wide, 0, 0)),
        out_shape=field,
        scratch_shapes=[pltpu.VMEM((deep + 2, wide + 2, size, 2 * sides), bf16)],
        compiler_params=params(16),
        cost_estimate=cost(12),
        name="near",
    )(
        col_near, col_cross, from_cross, from_near, row_near, row_cross, corner_near, corner_cross,
        near_blocks,
    )
    return pl.pallas_call(
        far_kernel,
        in_specs=[ANY, VMEM, VMEM, VMEM],
        out_specs=ANY,
        out_shape=field,
        scratch_shapes=[
            pltpu.VMEM(leaf_live.shape, jnp.int32),
            pltpu.VMEM((parts, block, 2 * sides), bf16),
            pltpu.VMEM(unknowns.shape, f32),
            pltpu.SemaphoreType.DMA,
            pltpu.SemaphoreType.DMA((deep, wide)),
        ],
        compiler_params=params(16),
        name="far",
    )(leaf_live, returned, disaggregate, near)


def solution(mesh):
    in_specs = (
        P(None, "sect", "dir", None, None),
        P("sect", "dir"),
        P(None, "sect", "dir", None, None, None),
        P(None, "sect", "dir", None, None),
        P(None, "sect", "dir", None, None),
        P(None, None, "dir"),
    )
    out_specs = P(None, "sect", "dir", None, None)
    return jax.shard_map(shards, mesh=mesh, in_specs=in_specs, out_specs=out_specs, check_vma=False)
```

```python
import jax
import jax.numpy as jnp
from jax import lax
from jax.experimental import pallas as pl
from jax.experimental.pallas import tpu as pltpu
from jax.sharding import PartitionSpec as P

REACH = 2
MIB = 1 << 20
far_offsets = [
    (row_step, col_step)
    for row_step in range(-REACH, REACH + 1)
    for col_step in range(-REACH, REACH + 1)
    if max(abs(row_step), abs(col_step)) == REACH
]
VMEM = pl.BlockSpec(memory_space=pltpu.VMEM)
ANY = pl.BlockSpec(memory_space=pl.ANY)


def params(mib=56):
    return pltpu.CompilerParams(vmem_limit_bytes=mib * MIB)


def cost(micros):
    return pl.CostEstimate(flops=int(micros * 1.15e9), bytes_accessed=int(micros * 3.69e6), transcendentals=0)


def swap_pairs(count, first):
    pairs = []
    for i in range(count):
        partner = i + 1 if (i - first) % 2 == 0 else i - 1
        pairs.append((i, partner if 0 <= partner < count else None))
    return pairs


def swap_cols(array, first):
    rows, cols = lax.axis_size("sect"), lax.axis_size("dir")
    sends = []
    for row in range(rows):
        for col, partner in swap_pairs(cols, first):
            to = (row ^ 1) * cols + col if partner is None else row * cols + partner
            sends.append((row * cols + col, to))
    return lax.ppermute(array, ("sect", "dir"), sends)


def swap_rows(array, first, turn=0):
    rows, cols = lax.axis_size("sect"), lax.axis_size("dir")
    sends = []
    for row, partner in swap_pairs(rows, first):
        for col in range(cols):
            to = row * cols + (col ^ 1) if partner is None else partner * cols + (col ^ turn)
            sends.append((row * cols + col, to))
    return lax.ppermute(array, ("sect", "dir"), sends)


def complex_dot(left_real, left_imag, right):
    rows = left_real.shape[0]
    cols = right.shape[1] // 2
    both = jnp.dot(
        jnp.concatenate([left_real, left_imag], axis=0), right, preferred_element_type=jnp.float32
    )
    real = both[:rows, :cols] - both[rows:, cols:]
    imag = both[:rows, cols:] + both[rows:, :cols]
    return real, imag


def pattern_kernel(
    live_ref, unknowns_ref, aggregate_ref, out_ref, near_ref, cross_ref, corner_near_ref,
    corner_cross_ref, leaves_ref,
):
    parts, _, narrow, sides = out_ref.shape
    deep, wide, size = unknowns_ref.shape[1:4]

    for u in range(deep):
        for v in range(wide):
            keep = live_ref[u, v].astype(jnp.float32).astype(jnp.bfloat16)
            at = (u * wide + v) * size
            for c in range(2):
                leaves_ref[at : at + size, c * sides : (c + 1) * sides] = (
                    unknowns_ref[c, u, v] * keep
                )

    left = [
        jnp.concatenate([aggregate_ref[c, u, v] for u in range(deep) for v in range(wide)], axis=1)
        for c in range(2)
    ]
    real, imag = complex_dot(left[0], left[1], leaves_ref[...])
    for part in range(parts):
        out_ref[part, 0] = real[part * narrow : (part + 1) * narrow].astype(jnp.bfloat16)
        out_ref[part, 1] = imag[part * narrow : (part + 1) * narrow].astype(jnp.bfloat16)

    odd = lax.rem(lax.axis_index("dir"), 2)
    row_odd = lax.rem(lax.axis_index("sect"), 2)

    def leaf(u, v, c):
        at = pl.multiple_of((u * wide + v) * size, size)
        return leaves_ref[pl.ds(at, size), c * sides : (c + 1) * sides]

    for c in range(2):
        for u in range(deep):
            near_ref[c, u] = leaf(u, 1 - odd, c)
            cross_ref[c, u] = leaf(u, odd, c)
        corner_near_ref[c] = leaf(1 - row_odd, 1 - odd, c)
        corner_cross_ref[c] = leaf(row_odd, 1 - odd, c)


def coefficient_kernel(coef_ref, wide_ref, turned_ref):
    _, _, narrow, lanes = wide_ref.shape
    turned_ref[...] = coef_ref[...].T
    first = pl.multiple_of(lax.axis_index("sect") * narrow, narrow)
    coefs = turned_ref[pl.ds(first, narrow)]
    for index in range(len(far_offsets)):
        real, imag = [
            jnp.broadcast_to(coefs[:, 2 * index + c : 2 * index + c + 1], (narrow, lanes)) for c in range(2)
        ]
        wide_ref[index, 0] = real
        wide_ref[index, 1] = imag
        wide_ref[index, 2] = real + imag


def translate_kernel(from_ref, wide_ref, out_ref, held_ref):
    box_cols, box_rows, _, narrow, sides = from_ref.shape
    lanes = min(128, sides)

    def tile(place, carry):
        across = pl.ds(pl.multiple_of(place * lanes, lanes), lanes)
        real = from_ref[:, :, 0, :, across].astype(jnp.float32)
        imag = from_ref[:, :, 1, :, across].astype(jnp.float32)
        held_ref[:, :, 0] = real
        held_ref[:, :, 1] = imag
        held_ref[:, :, 2] = real + imag
        for col in range(box_cols):
            totals = [None] * box_rows
            for source in range(box_rows):
                held = {
                    step: [held_ref[col + step, source, k] for k in range(3)]
                    for step in range(-REACH, REACH + 1)
                    if 0 <= col + step < box_cols
                }
                for target in range(max(0, source - REACH), min(box_rows, source + REACH + 1)):
                    sums = None
                    for index, (row_step, step) in enumerate(far_offsets):
                        if row_step == source - target and step in held:
                            terms = [wide_ref[index, k] * held[step][k] for k in range(3)]
                            sums = terms if sums is None else [x + y for x, y in zip(sums, terms)]
                    if sums is None:
                        continue
                    a, b, c = sums
                    term = [x.astype(jnp.bfloat16).astype(jnp.float32) for x in (a - b, c - a - b)]
                    old = totals[target]
                    totals[target] = term if old is None else [x + y for x, y in zip(old, term)]
            for target, total in enumerate(totals):
                for c in range(2):
                    out_ref[col, target, c, :, across] = (
                        jnp.zeros((narrow, lanes), jnp.bfloat16)
                        if total is None
                        else total[c].astype(jnp.bfloat16)
                    )
        return carry

    lax.fori_loop(0, sides // lanes, tile, 0, unroll=True)


def translate_grid(sources, coefs):
    box_rows, box_cols = sources.shape[:2]
    widened = jnp.pad(sources.astype(jnp.float32), ((REACH, REACH), (REACH, REACH), (0, 0), (0, 0), (0, 0)))
    accum = jnp.zeros(sources.shape, jnp.float32)
    for row_step in range(-REACH, REACH + 1):
        total = jnp.zeros(sources.shape, jnp.float32)
        for index, (step_row, step_col) in enumerate(far_offsets):
            if step_row == row_step:
                shifted = widened[
                    REACH + step_row : REACH + step_row + box_rows,
                    REACH + step_col : REACH + step_col + box_cols,
                ]
                coef_real = coefs[index, 0][None, None, :, None]
                coef_imag = coefs[index, 1][None, None, :, None]
                real = coef_real * shifted[:, :, 0] - coef_imag * shifted[:, :, 1]
                imag = coef_real * shifted[:, :, 1] + coef_imag * shifted[:, :, 0]
                total = total + jnp.stack([real, imag], axis=2)
        accum = accum + total.astype(jnp.bfloat16).astype(jnp.float32)
    return accum.astype(jnp.bfloat16)


def move(copies, sem):
    arrivals = [
        pltpu.make_async_copy(source, held, sem.at[0, i]) for i, (source, held, _) in enumerate(copies)
    ]
    departures = [
        pltpu.make_async_copy(held, target, sem.at[1, i]) for i, (_, held, target) in enumerate(copies)
    ]
    for copy in arrivals:
        copy.start()
    for arrival, departure in zip(arrivals, departures):
        arrival.wait()
        departure.start()
    for copy in departures:
        copy.wait()


def row_kernel(near_ref, cross_ref, from_cross_ref, out_near_ref, out_cross_ref, held_ref, sem):
    odd = lax.rem(lax.axis_index("sect"), 2)
    copies = []
    for slot, ref in enumerate((near_ref, cross_ref, from_cross_ref)):
        copies.append((ref.at[:, 1 - odd], held_ref.at[0, slot], out_near_ref.at[:, slot]))
        copies.append((ref.at[:, odd], held_ref.at[1, slot], out_cross_ref.at[:, slot]))
    move(copies, sem)


def near_kernel(
    near_ref, cross_ref, from_cross_ref, from_near_ref, row_near_ref, row_cross_ref, corner_near_ref,
    corner_cross_ref, blocks_ref, out_ref, grid_ref,
):
    sides = near_ref.shape[3]
    deep = near_ref.shape[1]
    wide = 2
    leaf = pl.program_id(0)

    @pl.when(leaf == 0)
    def _():
        col_at, col_count = lax.axis_index("dir"), lax.axis_size("dir")
        row_at, row_count = lax.axis_index("sect"), lax.axis_size("sect")
        col_odd, row_odd = lax.rem(col_at, 2), lax.rem(row_at, 2)
        columns = (2 - col_odd, 1 + col_odd, 3 * col_odd, 3 - 3 * col_odd)
        row_next, row_last = 3 - 3 * row_odd, 3 * row_odd
        no_col = ((col_odd == 0) & (col_at == 0)) | ((col_odd == 1) & (col_at == col_count - 1))
        no_row = ((row_odd == 0) & (row_at == 0)) | ((row_odd == 1) & (row_at == row_count - 1))
        for slot, ref in enumerate((near_ref, cross_ref, from_cross_ref, from_near_ref)):
            for c in range(2):
                half = slice(c * sides, (c + 1) * sides)
                for u in range(deep):
                    grid_ref[1 + u, columns[slot], :, half] = ref[c, u]
                if slot < 3:
                    grid_ref[row_next, columns[slot], :, half] = row_near_ref[c, slot]
                    grid_ref[row_last, columns[slot], :, half] = row_cross_ref[c, slot]
                else:
                    grid_ref[row_next, columns[slot], :, half] = corner_near_ref[c]
                    grid_ref[row_last, columns[slot], :, half] = corner_cross_ref[c]

        @pl.when(no_col)
        def _():
            for i in range(deep + 2):
                grid_ref[i, columns[2]] = jnp.zeros(grid_ref.shape[2:], grid_ref.dtype)

        @pl.when(no_row)
        def _():
            for j in range(wide + 2):
                grid_ref[row_last, j] = jnp.zeros(grid_ref.shape[2:], grid_ref.dtype)

    u, v = leaf // wide, lax.rem(leaf, wide)
    right = jnp.concatenate(
        [grid_ref[u + a, v + b] for a in range(3) for b in range(3)], axis=0
    )
    left = [jnp.concatenate([blocks_ref[c, 0, 0, k] for k in range(9)], axis=1) for c in range(2)]
    real, imag = complex_dot(left[0], left[1], right)
    out_ref[0, 0, 0] = real
    out_ref[1, 0, 0] = imag


def far_kernel(
    live_ref, incoming_ref, disaggregate_ref, near_ref, out_ref, live_here, right_ref, made_ref, live_sem,
    out_sem,
):
    parts, _, narrow, sides = incoming_ref.shape
    deep, wide = live_ref.shape

    def departure(u, v):
        return pltpu.make_async_copy(
            made_ref.at[:, u, v], out_ref.at[:, u, v], out_sem.at[u, v]
        )

    live_copy = pltpu.make_async_copy(live_ref, live_here, live_sem)
    live_copy.start()
    for c in range(2):
        right_ref[:, :, c * sides : (c + 1) * sides] = incoming_ref[:, c]
    live_copy.wait()
    right = right_ref[...].reshape(parts * narrow, 2 * sides)
    for u in range(deep):
        for v in range(wide):
            live = live_here[u : u + 1, v : v + 1].astype(jnp.float32)
            real, imag = complex_dot(disaggregate_ref[0, u, v], disaggregate_ref[1, u, v], right)
            made_ref[0, u, v] = (near_ref[0, u, v] + real) * live
            made_ref[1, u, v] = (near_ref[1, u, v] + imag) * live
            departure(u, v).start()
    for u in range(deep):
        for v in range(wide):
            departure(u, v).wait()


def shards(unknowns, leaf_live, near_blocks, aggregate, disaggregate, translate):
    sect_count, dir_count = lax.axis_size("sect"), lax.axis_size("dir")
    _, deep, wide, size, sides = unknowns.shape
    total_dirs = aggregate.shape[3]
    narrow = total_dirs // (sect_count * dir_count)
    held = translate.shape[2]
    bf16, f32 = jnp.bfloat16, jnp.float32
    tiled = narrow % 16 == 0
    parts = dir_count * sect_count if tiled else 1
    block = total_dirs // parts

    column = jax.ShapeDtypeStruct((2, deep, size, sides), bf16)
    corner = jax.ShapeDtypeStruct((2, size, sides), bf16)
    blocks = jax.ShapeDtypeStruct((parts, 2, block, sides), bf16)
    patterns, col_near, col_cross, corner_near, corner_cross = pl.pallas_call(
        pattern_kernel,
        in_specs=[pl.BlockSpec(memory_space=pltpu.SMEM), VMEM, VMEM],
        out_specs=[VMEM] * 5,
        out_shape=[blocks, column, column, corner, corner],
        scratch_shapes=[pltpu.VMEM((deep * wide * size, 2 * sides), bf16)],
        compiler_params=params(),
        name="patterns",
    )(leaf_live, unknowns, aggregate)
    from_cross = swap_cols(col_cross, 1)
    from_near = swap_cols(col_near, 0)
    corner_near = swap_rows(corner_near, 0, 1)
    corner_cross = swap_rows(corner_cross, 1, 1)

    row = jax.ShapeDtypeStruct((2, 3, size, sides), bf16)
    row_near, row_cross = pl.pallas_call(
        row_kernel,
        in_specs=[ANY] * 3,
        out_specs=[ANY] * 2,
        out_shape=[row, row],
        scratch_shapes=[
            pltpu.VMEM((2, 3, 2, size, sides), bf16),
            pltpu.SemaphoreType.DMA((2, 6)),
        ],
        compiler_params=params(),
        cost_estimate=cost(8),
        name="rows",
    )(col_near, col_cross, from_cross)

    def spread(array):
        flat = array.reshape(parts, 2, block, sides)
        return lax.all_to_all(flat, ("dir", "sect"), split_axis=0, concat_axis=0, tiled=True)

    if tiled:
        own = spread(patterns).reshape(dir_count, sect_count, 2, block, sides)
        lanes = min(128, sides)
        coefs, _ = lax.optimization_barrier((translate, row_cross))
        wide_coefs = pl.pallas_call(
            coefficient_kernel,
            in_specs=[VMEM],
            out_specs=VMEM,
            out_shape=jax.ShapeDtypeStruct((len(far_offsets), 3, narrow, lanes), f32),
            scratch_shapes=[pltpu.VMEM((held, 2 * len(far_offsets)), f32)],
            compiler_params=params(16),
            name="coefficients",
        )(coefs.reshape(2 * len(far_offsets), held))
        own, _, _, wide_coefs = lax.optimization_barrier((own, row_near, row_cross, wide_coefs))
        incoming = pl.pallas_call(
            translate_kernel,
            in_specs=[VMEM] * 2,
            out_specs=VMEM,
            out_shape=jax.ShapeDtypeStruct(own.shape, bf16),
            scratch_shapes=[
                pltpu.VMEM((dir_count, sect_count, 3, narrow, lanes), f32),
            ],
            compiler_params=params(16),
            cost_estimate=cost(8),
            name="translations",
        )(own, wide_coefs)
        returned = spread(incoming)
    else:
        base = patterns.reshape(2, dir_count, sect_count, narrow, sides).transpose(0, 2, 1, 3, 4)
        base = base.reshape(2, total_dirs, sides)[None, None]
        own = lax.all_to_all(base, "sect", split_axis=3, concat_axis=0, tiled=True)
        own = lax.all_to_all(own, "dir", split_axis=3, concat_axis=1, tiled=True)
        coefs = lax.dynamic_slice_in_dim(translate, lax.axis_index("sect") * narrow, narrow, 2)
        incoming = translate_grid(own, coefs)
        returned = lax.all_to_all(incoming, "sect", split_axis=0, concat_axis=3, tiled=True)
        returned = lax.all_to_all(returned, "dir", split_axis=1, concat_axis=3, tiled=True)[0]

    row_near = swap_rows(row_near, 0)
    row_cross = swap_rows(row_cross, 1)
    field = jax.ShapeDtypeStruct(unknowns.shape, f32)
    near = pl.pallas_call(
        near_kernel,
        grid=(deep * wide,),
        in_specs=[VMEM] * 8
        + [pl.BlockSpec((2, 1, 1, 9, size, size), lambda i: (0, i // wide, i % wide, 0, 0, 0))],
        out_specs=pl.BlockSpec((2, 1, 1, size, sides), lambda i: (0, i // wide, i % wide, 0, 0)),
        out_shape=field,
        scratch_shapes=[pltpu.VMEM((deep + 2, wide + 2, size, 2 * sides), bf16)],
        compiler_params=params(16),
        cost_estimate=cost(12),
        name="near",
    )(
        col_near, col_cross, from_cross, from_near, row_near, row_cross, corner_near, corner_cross,
        near_blocks,
    )
    return pl.pallas_call(
        far_kernel,
        in_specs=[ANY, VMEM, VMEM, VMEM],
        out_specs=ANY,
        out_shape=field,
        scratch_shapes=[
            pltpu.VMEM(leaf_live.shape, jnp.int32),
            pltpu.VMEM((parts, block, 2 * sides), bf16),
            pltpu.VMEM(unknowns.shape, f32),
            pltpu.SemaphoreType.DMA,
            pltpu.SemaphoreType.DMA((deep, wide)),
        ],
        compiler_params=params(16),
        name="far",
    )(leaf_live, returned, disaggregate, near)


def solution(mesh):
    in_specs = (
        P(None, "sect", "dir", None, None),
        P("sect", "dir"),
        P(None, "sect", "dir", None, None, None),
        P(None, "sect", "dir", None, None),
        P(None, "sect", "dir", None, None),
        P(None, None, "dir"),
    )
    out_specs = P(None, "sect", "dir", None, None)
    return jax.shard_map(shards, mesh=mesh, in_specs=in_specs, out_specs=out_specs, check_vma=False)
```

```python
import jax
import jax.numpy as jnp
from jax import lax
from jax.experimental import pallas as pl
from jax.experimental.pallas import tpu as pltpu
from jax.sharding import PartitionSpec as P

REACH = 2
MIB = 1 << 20
far_offsets = [
    (row_step, col_step)
    for row_step in range(-REACH, REACH + 1)
    for col_step in range(-REACH, REACH + 1)
    if max(abs(row_step), abs(col_step)) == REACH
]
VMEM = pl.BlockSpec(memory_space=pltpu.VMEM)
ANY = pl.BlockSpec(memory_space=pl.ANY)


def params(mib=56):
    return pltpu.CompilerParams(vmem_limit_bytes=mib * MIB)


def cost(micros):
    return pl.CostEstimate(flops=int(micros * 1.15e9), bytes_accessed=int(micros * 3.69e6), transcendentals=0)


def swap_pairs(count, first):
    pairs = []
    for i in range(count):
        partner = i + 1 if (i - first) % 2 == 0 else i - 1
        pairs.append((i, partner if 0 <= partner < count else None))
    return pairs


def swap_cols(array, first):
    rows, cols = lax.axis_size("sect"), lax.axis_size("dir")
    sends = []
    for row in range(rows):
        for col, partner in swap_pairs(cols, first):
            to = (row ^ 1) * cols + col if partner is None else row * cols + partner
            sends.append((row * cols + col, to))
    return lax.ppermute(array, ("sect", "dir"), sends)


def swap_rows(array, first, turn=0):
    rows, cols = lax.axis_size("sect"), lax.axis_size("dir")
    sends = []
    for row, partner in swap_pairs(rows, first):
        for col in range(cols):
            to = row * cols + (col ^ 1) if partner is None else partner * cols + (col ^ turn)
            sends.append((row * cols + col, to))
    return lax.ppermute(array, ("sect", "dir"), sends)


def complex_dot(left_real, left_imag, right):
    rows = left_real.shape[0]
    cols = right.shape[1] // 2
    both = jnp.dot(
        jnp.concatenate([left_real, left_imag], axis=0), right, preferred_element_type=jnp.float32
    )
    real = both[:rows, :cols] - both[rows:, cols:]
    imag = both[:rows, cols:] + both[rows:, :cols]
    return real, imag


def pattern_kernel(
    live_ref, unknowns_ref, aggregate_ref, out_ref, near_ref, cross_ref, corner_near_ref,
    corner_cross_ref, leaves_ref,
):
    parts, _, narrow, sides = out_ref.shape
    deep, wide, size = unknowns_ref.shape[1:4]

    for u in range(deep):
        for v in range(wide):
            keep = live_ref[u, v].astype(jnp.float32).astype(jnp.bfloat16)
            at = (u * wide + v) * size
            for c in range(2):
                leaves_ref[at : at + size, c * sides : (c + 1) * sides] = (
                    unknowns_ref[c, u, v] * keep
                )

    left = [
        jnp.concatenate([aggregate_ref[c, u, v] for u in range(deep) for v in range(wide)], axis=1)
        for c in range(2)
    ]
    real, imag = complex_dot(left[0], left[1], leaves_ref[...])
    for part in range(parts):
        out_ref[part, 0] = real[part * narrow : (part + 1) * narrow].astype(jnp.bfloat16)
        out_ref[part, 1] = imag[part * narrow : (part + 1) * narrow].astype(jnp.bfloat16)

    odd = lax.rem(lax.axis_index("dir"), 2)
    row_odd = lax.rem(lax.axis_index("sect"), 2)

    def leaf(u, v, c):
        at = pl.multiple_of((u * wide + v) * size, size)
        return leaves_ref[pl.ds(at, size), c * sides : (c + 1) * sides]

    for c in range(2):
        for u in range(deep):
            near_ref[c, u] = leaf(u, 1 - odd, c)
            cross_ref[c, u] = leaf(u, odd, c)
        corner_near_ref[c] = leaf(1 - row_odd, 1 - odd, c)
        corner_cross_ref[c] = leaf(row_odd, 1 - odd, c)


def coefficient_kernel(coef_ref, wide_ref, turned_ref):
    _, _, narrow, lanes = wide_ref.shape
    turned_ref[...] = coef_ref[...].T
    first = pl.multiple_of(lax.axis_index("sect") * narrow, narrow)
    coefs = turned_ref[pl.ds(first, narrow)]
    for index in range(len(far_offsets)):
        real, imag = [
            jnp.broadcast_to(coefs[:, 2 * index + c : 2 * index + c + 1], (narrow, lanes)) for c in range(2)
        ]
        wide_ref[index, 0] = real
        wide_ref[index, 1] = imag
        wide_ref[index, 2] = real + imag


def translate_kernel(from_ref, wide_ref, out_ref, held_ref, made_ref, sem):
    box_cols, box_rows, _, narrow, sides = from_ref.shape
    lanes = min(128, sides)

    def departure(place):
        across = pl.ds(pl.multiple_of(place * lanes, lanes), lanes)
        return pltpu.make_async_copy(made_ref.at[..., across], out_ref.at[..., across], sem.at[place])

    def tile(place, carry):
        across = pl.ds(pl.multiple_of(place * lanes, lanes), lanes)
        real = from_ref[:, :, 0, :, across].astype(jnp.float32)
        imag = from_ref[:, :, 1, :, across].astype(jnp.float32)
        held_ref[:, :, 0] = real
        held_ref[:, :, 1] = imag
        held_ref[:, :, 2] = real + imag
        for col in range(box_cols):
            totals = [None] * box_rows
            for source in range(box_rows):
                held = {
                    step: [held_ref[col + step, source, k] for k in range(3)]
                    for step in range(-REACH, REACH + 1)
                    if 0 <= col + step < box_cols
                }
                for target in range(max(0, source - REACH), min(box_rows, source + REACH + 1)):
                    sums = None
                    for index, (row_step, step) in enumerate(far_offsets):
                        if row_step == source - target and step in held:
                            terms = [wide_ref[index, k] * held[step][k] for k in range(3)]
                            sums = terms if sums is None else [x + y for x, y in zip(sums, terms)]
                    if sums is None:
                        continue
                    a, b, c = sums
                    term = [x.astype(jnp.bfloat16).astype(jnp.float32) for x in (a - b, c - a - b)]
                    old = totals[target]
                    totals[target] = term if old is None else [x + y for x, y in zip(old, term)]
            for target, total in enumerate(totals):
                for c in range(2):
                    made_ref[col, target, c, :, across] = (
                        jnp.zeros((narrow, lanes), jnp.bfloat16)
                        if total is None
                        else total[c].astype(jnp.bfloat16)
                    )
        departure(place).start()
        return carry

    lax.fori_loop(0, sides // lanes, tile, 0, unroll=True)
    for place in range(sides // lanes):
        departure(place).wait()


def translate_grid(sources, coefs):
    box_rows, box_cols = sources.shape[:2]
    widened = jnp.pad(sources.astype(jnp.float32), ((REACH, REACH), (REACH, REACH), (0, 0), (0, 0), (0, 0)))
    accum = jnp.zeros(sources.shape, jnp.float32)
    for row_step in range(-REACH, REACH + 1):
        total = jnp.zeros(sources.shape, jnp.float32)
        for index, (step_row, step_col) in enumerate(far_offsets):
            if step_row == row_step:
                shifted = widened[
                    REACH + step_row : REACH + step_row + box_rows,
                    REACH + step_col : REACH + step_col + box_cols,
                ]
                coef_real = coefs[index, 0][None, None, :, None]
                coef_imag = coefs[index, 1][None, None, :, None]
                real = coef_real * shifted[:, :, 0] - coef_imag * shifted[:, :, 1]
                imag = coef_real * shifted[:, :, 1] + coef_imag * shifted[:, :, 0]
                total = total + jnp.stack([real, imag], axis=2)
        accum = accum + total.astype(jnp.bfloat16).astype(jnp.float32)
    return accum.astype(jnp.bfloat16)


def move(copies, sem):
    arrivals = [
        pltpu.make_async_copy(source, held, sem.at[0, i]) for i, (source, held, _) in enumerate(copies)
    ]
    departures = [
        pltpu.make_async_copy(held, target, sem.at[1, i]) for i, (_, held, target) in enumerate(copies)
    ]
    for copy in arrivals:
        copy.start()
    for arrival, departure in zip(arrivals, departures):
        arrival.wait()
        departure.start()
    for copy in departures:
        copy.wait()


def row_kernel(near_ref, cross_ref, from_cross_ref, out_near_ref, out_cross_ref, held_ref, sem):
    odd = lax.rem(lax.axis_index("sect"), 2)
    copies = []
    for slot, ref in enumerate((near_ref, cross_ref, from_cross_ref)):
        copies.append((ref.at[:, 1 - odd], held_ref.at[0, slot], out_near_ref.at[:, slot]))
        copies.append((ref.at[:, odd], held_ref.at[1, slot], out_cross_ref.at[:, slot]))
    move(copies, sem)


def near_kernel(
    near_ref, cross_ref, from_cross_ref, from_near_ref, row_near_ref, row_cross_ref, corner_near_ref,
    corner_cross_ref, blocks_ref, out_ref, grid_ref,
):
    sides = near_ref.shape[3]
    deep = near_ref.shape[1]
    wide = 2
    leaf = pl.program_id(0)

    @pl.when(leaf == 0)
    def _():
        col_at, col_count = lax.axis_index("dir"), lax.axis_size("dir")
        row_at, row_count = lax.axis_index("sect"), lax.axis_size("sect")
        col_odd, row_odd = lax.rem(col_at, 2), lax.rem(row_at, 2)
        columns = (2 - col_odd, 1 + col_odd, 3 * col_odd, 3 - 3 * col_odd)
        row_next, row_last = 3 - 3 * row_odd, 3 * row_odd
        no_col = ((col_odd == 0) & (col_at == 0)) | ((col_odd == 1) & (col_at == col_count - 1))
        no_row = ((row_odd == 0) & (row_at == 0)) | ((row_odd == 1) & (row_at == row_count - 1))
        for slot, ref in enumerate((near_ref, cross_ref, from_cross_ref, from_near_ref)):
            for c in range(2):
                half = slice(c * sides, (c + 1) * sides)
                for u in range(deep):
                    grid_ref[1 + u, columns[slot], :, half] = ref[c, u]
                if slot < 3:
                    grid_ref[row_next, columns[slot], :, half] = row_near_ref[c, slot]
                    grid_ref[row_last, columns[slot], :, half] = row_cross_ref[c, slot]
                else:
                    grid_ref[row_next, columns[slot], :, half] = corner_near_ref[c]
                    grid_ref[row_last, columns[slot], :, half] = corner_cross_ref[c]

        @pl.when(no_col)
        def _():
            for i in range(deep + 2):
                grid_ref[i, columns[2]] = jnp.zeros(grid_ref.shape[2:], grid_ref.dtype)

        @pl.when(no_row)
        def _():
            for j in range(wide + 2):
                grid_ref[row_last, j] = jnp.zeros(grid_ref.shape[2:], grid_ref.dtype)

    u, v = leaf // wide, lax.rem(leaf, wide)
    right = jnp.concatenate(
        [grid_ref[u + a, v + b] for a in range(3) for b in range(3)], axis=0
    )
    left = [jnp.concatenate([blocks_ref[c, 0, 0, k] for k in range(9)], axis=1) for c in range(2)]
    real, imag = complex_dot(left[0], left[1], right)
    out_ref[0, 0, 0] = real
    out_ref[1, 0, 0] = imag


def far_kernel(
    live_ref, incoming_ref, disaggregate_ref, near_ref, out_ref, live_here, right_ref, made_ref, live_sem,
    out_sem,
):
    parts, _, narrow, sides = incoming_ref.shape
    deep, wide = live_ref.shape

    def departure(u, v):
        return pltpu.make_async_copy(
            made_ref.at[:, u, v], out_ref.at[:, u, v], out_sem.at[u, v]
        )

    live_copy = pltpu.make_async_copy(live_ref, live_here, live_sem)
    live_copy.start()
    for c in range(2):
        right_ref[:, :, c * sides : (c + 1) * sides] = incoming_ref[:, c]
    live_copy.wait()
    right = right_ref[...].reshape(parts * narrow, 2 * sides)
    for u in range(deep):
        for v in range(wide):
            live = live_here[u : u + 1, v : v + 1].astype(jnp.float32)
            real, imag = complex_dot(disaggregate_ref[0, u, v], disaggregate_ref[1, u, v], right)
            made_ref[0, u, v] = (near_ref[0, u, v] + real) * live
            made_ref[1, u, v] = (near_ref[1, u, v] + imag) * live
            departure(u, v).start()
    for u in range(deep):
        for v in range(wide):
            departure(u, v).wait()


def shards(unknowns, leaf_live, near_blocks, aggregate, disaggregate, translate):
    sect_count, dir_count = lax.axis_size("sect"), lax.axis_size("dir")
    _, deep, wide, size, sides = unknowns.shape
    total_dirs = aggregate.shape[3]
    narrow = total_dirs // (sect_count * dir_count)
    held = translate.shape[2]
    bf16, f32 = jnp.bfloat16, jnp.float32
    tiled = narrow % 16 == 0
    parts = dir_count * sect_count if tiled else 1
    block = total_dirs // parts

    column = jax.ShapeDtypeStruct((2, deep, size, sides), bf16)
    corner = jax.ShapeDtypeStruct((2, size, sides), bf16)
    blocks = jax.ShapeDtypeStruct((parts, 2, block, sides), bf16)
    patterns, col_near, col_cross, corner_near, corner_cross = pl.pallas_call(
        pattern_kernel,
        in_specs=[pl.BlockSpec(memory_space=pltpu.SMEM), VMEM, VMEM],
        out_specs=[VMEM] * 5,
        out_shape=[blocks, column, column, corner, corner],
        scratch_shapes=[pltpu.VMEM((deep * wide * size, 2 * sides), bf16)],
        compiler_params=params(),
        name="patterns",
    )(leaf_live, unknowns, aggregate)
    from_cross = swap_cols(col_cross, 1)
    from_near = swap_cols(col_near, 0)
    corner_near = swap_rows(corner_near, 0, 1)
    corner_cross = swap_rows(corner_cross, 1, 1)

    row = jax.ShapeDtypeStruct((2, 3, size, sides), bf16)
    row_near, row_cross = pl.pallas_call(
        row_kernel,
        in_specs=[ANY] * 3,
        out_specs=[ANY] * 2,
        out_shape=[row, row],
        scratch_shapes=[
            pltpu.VMEM((2, 3, 2, size, sides), bf16),
            pltpu.SemaphoreType.DMA((2, 6)),
        ],
        compiler_params=params(),
        cost_estimate=cost(8),
        name="rows",
    )(col_near, col_cross, from_cross)

    def spread(array):
        flat = array.reshape(parts, 2, block, sides)
        return lax.all_to_all(flat, ("dir", "sect"), split_axis=0, concat_axis=0, tiled=True)

    if tiled:
        own = spread(patterns).reshape(dir_count, sect_count, 2, block, sides)
        lanes = min(128, sides)
        coefs, _ = lax.optimization_barrier((translate, row_cross))
        wide_coefs = pl.pallas_call(
            coefficient_kernel,
            in_specs=[VMEM],
            out_specs=VMEM,
            out_shape=jax.ShapeDtypeStruct((len(far_offsets), 3, narrow, lanes), f32),
            scratch_shapes=[pltpu.VMEM((held, 2 * len(far_offsets)), f32)],
            compiler_params=params(16),
            name="coefficients",
        )(coefs.reshape(2 * len(far_offsets), held))
        own, _, _, wide_coefs = lax.optimization_barrier((own, row_near, row_cross, wide_coefs))
        incoming = pl.pallas_call(
            translate_kernel,
            in_specs=[VMEM] * 2,
            out_specs=ANY,
            out_shape=jax.ShapeDtypeStruct(own.shape, bf16),
            scratch_shapes=[
                pltpu.VMEM((dir_count, sect_count, 3, narrow, lanes), f32),
                pltpu.VMEM(own.shape, bf16),
                pltpu.SemaphoreType.DMA((sides // lanes,)),
            ],
            compiler_params=params(16),
            cost_estimate=cost(8),
            name="translations",
        )(own, wide_coefs)
        returned = spread(incoming)
    else:
        base = patterns.reshape(2, dir_count, sect_count, narrow, sides).transpose(0, 2, 1, 3, 4)
        base = base.reshape(2, total_dirs, sides)[None, None]
        own = lax.all_to_all(base, "sect", split_axis=3, concat_axis=0, tiled=True)
        own = lax.all_to_all(own, "dir", split_axis=3, concat_axis=1, tiled=True)
        coefs = lax.dynamic_slice_in_dim(translate, lax.axis_index("sect") * narrow, narrow, 2)
        incoming = translate_grid(own, coefs)
        returned = lax.all_to_all(incoming, "sect", split_axis=0, concat_axis=3, tiled=True)
        returned = lax.all_to_all(returned, "dir", split_axis=1, concat_axis=3, tiled=True)[0]

    row_near = swap_rows(row_near, 0)
    row_cross = swap_rows(row_cross, 1)
    field = jax.ShapeDtypeStruct(unknowns.shape, f32)
    near = pl.pallas_call(
        near_kernel,
        grid=(deep * wide,),
        in_specs=[VMEM] * 8
        + [pl.BlockSpec((2, 1, 1, 9, size, size), lambda i: (0, i // wide, i % wide, 0, 0, 0))],
        out_specs=pl.BlockSpec((2, 1, 1, size, sides), lambda i: (0, i // wide, i % wide, 0, 0)),
        out_shape=field,
        scratch_shapes=[pltpu.VMEM((deep + 2, wide + 2, size, 2 * sides), bf16)],
        compiler_params=params(16),
        cost_estimate=cost(12),
        name="near",
    )(
        col_near, col_cross, from_cross, from_near, row_near, row_cross, corner_near, corner_cross,
        near_blocks,
    )
    return pl.pallas_call(
        far_kernel,
        in_specs=[ANY, VMEM, VMEM, VMEM],
        out_specs=ANY,
        out_shape=field,
        scratch_shapes=[
            pltpu.VMEM(leaf_live.shape, jnp.int32),
            pltpu.VMEM((parts, block, 2 * sides), bf16),
            pltpu.VMEM(unknowns.shape, f32),
            pltpu.SemaphoreType.DMA,
            pltpu.SemaphoreType.DMA((deep, wide)),
        ],
        compiler_params=params(16),
        name="far",
    )(leaf_live, returned, disaggregate, near)


def solution(mesh):
    in_specs = (
        P(None, "sect", "dir", None, None),
        P("sect", "dir"),
        P(None, "sect", "dir", None, None, None),
        P(None, "sect", "dir", None, None),
        P(None, "sect", "dir", None, None),
        P(None, None, "dir"),
    )
    out_specs = P(None, "sect", "dir", None, None)
    return jax.shard_map(shards, mesh=mesh, in_specs=in_specs, out_specs=out_specs, check_vma=False)
```
